512 devices in a mesh: dp: 64 (over y, x, core), pair: 8 (over z).
Axes of the slice: x: 4, y: 8, z: 8, core: 2. Of those that a mesh axis runs over, the one named last changes fastest.
Arguments:
- documents: bfloat16 [524288, 1024], P(('dp', 'pair'))
- counts: int32 [512, 64], P(('dp', 'pair')), may hold values from 1 to 32, 1024 in all within a row
- neighbours: int32 [512, 3], P(('dp', 'pair')), may hold values from 0 to 3, as said below
Outputs:
- best_match: float32 [524288], P(('dp', 'pair'))
The draws below stay inside these ranges and needn't reach their ends.
Inputs may be any that keep to these rules, and one draw needn't show every extreme that they name: Row s of counts sums to 1024 and its largest entry is exactly 32. `neighbours`: the entries of one row differ.
All inputs are finite; a program needn't handle non-finite values.
Results may differ from the reference program's by a relative error of at most 0.0005.
Values may be sent and summed in bfloat16 or wider, within the bound.
No kernel may reach another device: no remote copies, remote signals or barrier semaphores. Data moves between devices by JAX's collectives and lax.ppermute only.
A program may use at most 128 MiB of HBM per device.

```python
import math
import jax
import jax.numpy as jnp
import numpy as np
from jax import lax

D = 1024
BLOCK = 512
NEIGHBOURS = 3
TOPICS = 1024
SLAB = 2048
CAP = 32
ROWS_DEV = 1024
SHARDS = 512
CLUSTERS = 512
DOCS = 524288
N_DP = 64
N_PAIR = 8


def draw_documents(key, part):
    key = jax.random.fold_in(key, 11)
    key_bank, key_topic, key_noise, key_scale, key_common, key_rare = jax.random.split(key, 6)
    bank = jax.random.normal(key_bank, (TOPICS, D), jnp.float32)
    topic = jax.random.randint(key_topic, (DOCS,), 0, TOPICS)
    common = jax.random.normal(key_common, (1, D), jnp.float32)
    opposite = jax.random.randint(key_rare, (DOCS, 1), 0, 4 * SLAB) == 0
    noise = jax.random.normal(key_noise, (DOCS, D), jnp.float32)
    scale = jnp.exp(jax.random.uniform(key_scale, (DOCS, 1), jnp.float32, 0.0, math.log(10.0)))
    along = 0.7
    against = 3.0
    drawn = noise + 0.8 * jnp.take(bank, topic, axis=0) + along * common
    contrary = noise - against * common
    mixed = jnp.where(opposite, contrary, drawn)
    return (scale * mixed).astype(jnp.bfloat16)


def draw_neighbours(key, part):
    key = jax.random.fold_in(key, 23)
    keys = jax.random.split(key, CLUSTERS)
    orders = jax.vmap(lambda one_key: jax.random.permutation(one_key, SLAB // BLOCK))(keys)
    return orders[:, :NEIGHBOURS].astype(jnp.int32)


def length_profile(amount, total, limit, skew):
    portions = [(1 << 20) // math.isqrt(standing ** skew) + 1 for standing in range(2, amount + 1)]
    rest, given = total - limit - (amount - 1), [1] * (amount - 1)
    while rest > 0:
        candidates = [i for i in range(amount - 1) if given[i] < limit]
        mass, remaining = sum([portions[i] for i in candidates]), rest
        for i in candidates:
            more = min(limit - given[i], max(1, remaining * portions[i] // mass), rest)
            given[i] = given[i] + more
            rest = rest - more
    return np.array([limit] + given)


def uneven_parts(own_key, count, total, limit, lean):
    if count == 2:
        one = jax.random.randint(own_key, (), max(1, total - limit), min(limit, total - 1) + 1)
        return jnp.stack([one, total - one])
    lengths = jnp.asarray(length_profile(count, total, limit, lean), jnp.int32)
    pairs = (count - 1) // 2
    donor, receiver = lengths[1:1 + 2 * pairs:2], lengths[2:2 + 2 * pairs:2]
    slack = jnp.minimum(donor - 1, limit - receiver)
    shifted = jax.random.randint(jax.random.fold_in(own_key, 1), (pairs,), 0, 1 << 20) % (slack + 1)
    lengths = lengths.at[1:1 + 2 * pairs:2].set(donor - shifted).at[2:2 + 2 * pairs:2].set(receiver + shifted)
    return lengths[jax.random.permutation(jax.random.fold_in(own_key, 2), count)]


def setup_inputs(seed: int = 0) -> dict:
    arg_keys = jax.random.split(jax.random.key(seed), 4)
    return {
        "documents": draw_documents(jax.random.fold_in(arg_keys[3], 71), 0),
        "counts": jax.vmap(lambda own: uneven_parts(own, N_DP, ROWS_DEV, CAP, 2))(jax.random.split(arg_keys[1], SHARDS)).reshape((SHARDS, N_DP)).astype(jnp.int32),
        "neighbours": draw_neighbours(jax.random.fold_in(arg_keys[3], 71), 0),
    }


floor_value = -2.0

def normalize(matrix):
    values = matrix.astype(jnp.float32)
    scaled = values * lax.rsqrt(lax.optimization_barrier(jnp.mean(values * values, axis=-1, keepdims=True)) + 1e-06)
    return scaled.astype(jnp.bfloat16)

def reference(documents, counts, neighbours):
    capacity = SLAB // N_DP
    lanes = SLAB // BLOCK
    unit_rows = normalize(documents).reshape(N_DP, N_PAIR, ROWS_DEV, D)
    count_grid = counts.reshape(N_DP, N_PAIR, N_DP)
    row_ends = jnp.cumsum(count_grid, axis=2)
    row_starts = row_ends - count_grid
    lane_index = jnp.arange(capacity, dtype=jnp.int32)
    listed = neighbours.reshape(N_DP, N_PAIR, NEIGHBOURS)

    def pick_rows(shard_rows, wanted):
        return jnp.take(shard_rows, wanted, axis=0)

    def one_owner(owner_index):
        start_here = lax.dynamic_index_in_dim(row_starts, owner_index, 2, keepdims=False)
        count_here = lax.dynamic_index_in_dim(count_grid, owner_index, 2, keepdims=False)
        wanted = jnp.clip(start_here[:, :, None] + lane_index[None, None, :], 0, ROWS_DEV - 1).astype(jnp.int32)
        usable = lane_index[None, None, :] < count_here[:, :, None]
        picked = jax.vmap(jax.vmap(pick_rows))(unit_rows, wanted)
        picked = jnp.where(usable[..., None], picked, jnp.zeros((), jnp.bfloat16))
        slab_rows = picked.transpose(1, 0, 2, 3).reshape(N_PAIR, SLAB, D).astype(jnp.float32)
        slot_ok = usable.transpose(1, 0, 2).reshape(N_PAIR, SLAB)
        choices_here = lax.dynamic_index_in_dim(listed, owner_index, 0, keepdims=False)
        best_rows = jnp.full((N_PAIR, SLAB), floor_value, jnp.float32)
        for neighbour in range(NEIGHBOURS):
            offset = 1 + neighbour % (N_PAIR - 1)
            block_start = (choices_here[:, neighbour] * BLOCK).astype(jnp.int32)
            block_rows = jax.vmap(lambda rows_in, begin: lax.dynamic_slice_in_dim(rows_in, begin, BLOCK, 0))(slab_rows, block_start)
            block_ok = jax.vmap(lambda ok_in, begin: lax.dynamic_slice_in_dim(ok_in, begin, BLOCK, 0))(slot_ok, block_start)
            target_rows = jnp.roll(slab_rows, -offset, axis=0)
            target_ok = jnp.roll(slot_ok, -offset, axis=0)
            scores = jnp.einsum('psd,pbd->psb', target_rows, block_rows) * (1.0 / D)
            scores = jnp.where(target_ok[:, :, None] & block_ok[:, None, :], scores, floor_value)
            best_rows = jnp.maximum(best_rows, jnp.roll(scores.max(axis=2), offset, axis=0))
            column_best = scores.max(axis=1)
            hit = jnp.arange(lanes, dtype=jnp.int32)[None, :] == choices_here[:, neighbour:neighbour + 1]
            extra = jnp.where(hit[:, :, None], column_best[:, None, :], floor_value).reshape(N_PAIR, SLAB)
            best_rows = jnp.maximum(best_rows, extra)
        return best_rows
    slab_best = lax.map(one_owner, jnp.arange(N_DP, dtype=jnp.int32))
    position = jnp.arange(ROWS_DEV, dtype=jnp.int32)
    owner_of = lax.optimization_barrier(jnp.sum((position[None, None, :, None] >= row_ends[:, :, None, :]).astype(jnp.int32), axis=3))
    rank_in = position[None, None, :] - jnp.take_along_axis(row_starts, owner_of, axis=2)
    shard_s = jnp.arange(N_DP, dtype=jnp.int32)[:, None, None]
    shard_p = jnp.arange(N_PAIR, dtype=jnp.int32)[None, :, None]
    flat_index = (owner_of * N_PAIR + shard_p) * SLAB + shard_s * capacity + rank_in
    return jnp.take(slab_best.reshape(-1), flat_index.reshape(-1).astype(jnp.int32))
```

```python
import functools

import jax
import jax.numpy as jnp
from jax import lax
from jax.experimental import pallas as pl
from jax.experimental.pallas import tpu as pltpu
from jax.sharding import PartitionSpec as P

BLOCK = 512
NEIGHBOURS = 3
SLAB = 2048
WIDTHS = (16, 16)
RELAYED = (256, 160)
PARTS = len(WIDTHS)
CHUNK = 256
FLOOR = -2.0
DEAD = -1e9
MARK = 64.0
MEBIBYTE = 1024 * 1024
MOST_VMEM = 60 * MEBIBYTE

NT = (((1,), (1,)), ((), ()))


def column_starts(counts_row, owner_column):
    owners = lax.broadcasted_iota(jnp.int32, (owner_column.shape[0], counts_row.shape[1]), 1)
    before = jnp.sum(jnp.where(owners < owner_column, counts_row, 0.0), axis=1, keepdims=True)
    own = jnp.sum(jnp.where(owners == owner_column, counts_row, 0.0), axis=1, keepdims=True)
    return before, own


def picked_rows(counts_row, unit_ref, start, tile, first, width):
    slot = lax.broadcasted_iota(jnp.int32, (tile, 1), 0) + start
    owner = lax.shift_right_logical(slot, width.bit_length() - 1)
    rank = (lax.bitwise_and(slot, width - 1) + first).astype(jnp.float32)
    before, own = column_starts(counts_row, owner)
    live = rank < own
    wanted = jnp.where(live, before + rank, -1.0).astype(jnp.int32)
    lane = lax.broadcasted_iota(jnp.int32, (tile, unit_ref.shape[0]), 1)
    choice = jnp.where(lane == wanted, 1.0, 0.0).astype(jnp.bfloat16)
    picked = jnp.dot(choice, unit_ref[...], preferred_element_type=jnp.float32)
    place = lax.broadcasted_iota(jnp.int32, (tile, picked.shape[1]), 1)
    return jnp.where((place == 0) & (wanted < 0), MARK, picked).astype(jnp.bfloat16)


def first_kernel(counts_ref, documents_ref, unit_out, part_out, raw, unit, part, in_sem, unit_sem, part_sem, *, width):
    tile = 128
    steps = raw.shape[0] // tile
    loads = []
    for step in range(steps):
        here = pl.ds(step * tile, tile)
        loads.append(pltpu.make_async_copy(documents_ref.at[here], raw.at[here], in_sem.at[step]))
        loads[-1].start()
    for step in range(steps):
        here = pl.ds(step * tile, tile)
        loads[step].wait()
        values = raw[here, :].astype(jnp.float32)
        mean = jnp.mean(values * values, axis=-1, keepdims=True)
        unit[here, :] = (values * lax.rsqrt(mean + 1e-06)).astype(jnp.bfloat16)
    stores = [pltpu.make_async_copy(unit, unit_out, unit_sem)]
    stores[-1].start()
    counts_row = counts_ref[...].astype(jnp.float32)
    tile = 256
    for step in range(part.shape[0] // tile):
        here = pl.ds(step * tile, tile)
        part[here, :] = picked_rows(counts_row, unit, step * tile, tile, 0, width)
        stores.append(pltpu.make_async_copy(part.at[here], part_out.at[here], part_sem.at[step]))
        stores[-1].start()
    for store in stores:
        store.wait()


def later_kernel(counts_ref, unit_ref, out_ref, *, first, width):
    counts_row = counts_ref[...].astype(jnp.float32)
    tile = 256

    @pl.loop(0, out_ref.shape[0] // tile)
    def _(step):
        here = pl.ds(pl.multiple_of(step * tile, tile), tile)
        out_ref[here, :] = picked_rows(counts_row, unit_ref, step * tile, tile, first, width)


def outgoing_parts(counts, documents):
    owners = counts.shape[1]
    rows, feats = documents.shape
    width = WIDTHS[0]
    size = owners * width
    shape = lambda n: jax.ShapeDtypeStruct((n, feats), jnp.bfloat16)
    cost = lambda n: pl.CostEstimate(
        flops=2 * n * rows * feats, bytes_accessed=2 * (n + rows) * feats, transcendentals=0
    )
    whole = pl.BlockSpec(memory_space=pltpu.VMEM)
    anywhere = pl.BlockSpec(memory_space=pltpu.HBM)
    unit, part = pl.pallas_call(
        functools.partial(first_kernel, width=width),
        out_shape=(shape(rows), shape(size)),
        in_specs=[whole, anywhere],
        out_specs=(anywhere, anywhere),
        scratch_shapes=[
            pltpu.VMEM((rows, feats), jnp.bfloat16),
            pltpu.VMEM((rows, feats), jnp.bfloat16),
            pltpu.VMEM((size, feats), jnp.bfloat16),
            pltpu.SemaphoreType.DMA((rows // 128,)),
            pltpu.SemaphoreType.DMA,
            pltpu.SemaphoreType.DMA((size // 256,)),
        ],
        compiler_params=pltpu.CompilerParams(vmem_limit_bytes=MOST_VMEM),
        cost_estimate=cost(size),
        name="unit_and_pick",
    )(counts, documents)
    parts = [part]
    first = width
    for width in WIDTHS[1:]:
        parts.append(
            pl.pallas_call(
                functools.partial(later_kernel, first=first, width=width),
                out_shape=shape(owners * width),
                in_specs=[whole, whole],
                out_specs=whole,
                compiler_params=pltpu.CompilerParams(vmem_limit_bytes=24 * MEBIBYTE),
                cost_estimate=cost(owners * width),
                name="pick",
            )(counts, unit)
        )
        first += width
    return parts


def score_tile(scores, row_bias, column_bias, best_ref, rows):
    live = scores + row_bias
    part = best_ref[rows, :]
    for lane in range(0, scores.shape[1], 128):
        part = jnp.maximum(part, live[:, lane : lane + 128])
    best_ref[rows, :] = part
    return jnp.max(scores + column_bias, axis=0, keepdims=True)


def block_bias(block):
    return jnp.where(block[:, 0:1].astype(jnp.float32) > 0.75 * MARK, DEAD, 0.0)


def best_row(best_ref, rows):
    turned = best_ref[rows, :].T
    return jnp.max(turned, axis=0, keepdims=True)


def row_offsets(refs):
    offsets = [0]
    for ref in refs:
        offsets.append(offsets[-1] + ref.shape[0])
    return offsets


def loads_of(refs, target, sems):
    offsets = row_offsets(refs)
    return [
        pltpu.make_async_copy(ref, target.at[pl.ds(offset, ref.shape[0])], sems.at[i])
        for i, (ref, offset) in enumerate(zip(refs, offsets))
    ]


def fold_scores(slab_refs, slab_loads, slab, blocks, best, row_bias_of, slab_best_of, slab_best_ref):
    tile = 256
    for index, offset in enumerate(row_offsets(slab_refs)[:-1]):
        slab_loads[index].wait()

        @pl.loop(0, slab_refs[index].shape[0] // tile)
        def _(step, offset=offset):
            there = pl.ds(pl.multiple_of(offset + step * tile, tile), tile)
            row_bias = row_bias_of(there)
            slab_best = slab_best_of(there)
            for begin in range(0, blocks.shape[0], CHUNK):
                rows = pl.ds(begin, CHUNK)
                block = blocks[rows, :]
                scores = lax.dot_general(block, slab[there, :], NT, preferred_element_type=jnp.float32)
                slab_best = jnp.maximum(
                    slab_best, score_tile(scores, row_bias, block_bias(block), best, rows)
                )
            slab_best_ref[:, there] = slab_best

    return jnp.concatenate(
        [best_row(best, pl.ds(begin, CHUNK)) for begin in range(0, blocks.shape[0], CHUNK)], axis=1
    )


def score_kernel(*refs, count, first):
    slab_refs, block_refs = refs[:PARTS], refs[PARTS : PARTS + count]
    refs = refs[PARTS + count :]
    if first:
        slab_best_ref, block_best_ref, row_bias_ref, slab, blocks, best, slab_sem, block_sem = refs
    else:
        row_bias_ref, before_ref, slab_best_ref, block_best_ref, slab, blocks, best, slab_sem, block_sem = refs
    block_loads = loads_of(block_refs, blocks, block_sem)
    slab_loads = loads_of(slab_refs, slab, slab_sem)
    for load in block_loads + slab_loads:
        load.start()
    best[...] = jnp.full(best.shape, 4 * DEAD, jnp.float32)
    for load in block_loads:
        load.wait()

    def row_bias_of(there):
        if not first:
            return row_bias_ref[:, there]
        marks = slab[there, 0:128].astype(jnp.float32).T[0:1, :]
        row_bias = jnp.where(marks > 0.75 * MARK, DEAD, 0.0)
        row_bias_ref[:, there] = row_bias
        return row_bias

    def slab_best_of(there):
        if not first:
            return before_ref[:, there]
        return jnp.full((1, there.size), FLOOR * 1024.0, jnp.float32)

    block_best_ref[...] = fold_scores(
        slab_refs, slab_loads, slab, blocks, best, row_bias_of, slab_best_of, slab_best_ref
    )


def score_scratch(slots, total, feats, blocks):
    return [
        pltpu.VMEM((slots, feats), jnp.bfloat16),
        pltpu.VMEM((total, feats), jnp.bfloat16),
        pltpu.VMEM((total, 128), jnp.float32),
        pltpu.SemaphoreType.DMA((PARTS,)),
        pltpu.SemaphoreType.DMA((blocks,)),
    ]


def score_cost(slots, total, feats):
    return pl.CostEstimate(
        flops=2 * slots * total * feats, bytes_accessed=2 * (slots + total) * feats, transcendentals=0
    )


def fold_blocks(slab_parts, blocks, before, name):
    feats = slab_parts[0].shape[1]
    whole = pl.BlockSpec(memory_space=pltpu.VMEM)
    anywhere = pl.BlockSpec(memory_space=pl.ANY)
    total = sum(block.shape[0] for block in blocks)
    row = lambda n: jax.ShapeDtypeStruct((1, n), jnp.float32)
    shapes = (row(SLAB), row(total)) if before else (row(SLAB), row(total), row(SLAB))
    return pl.pallas_call(
        functools.partial(score_kernel, count=len(blocks), first=not before),
        out_shape=shapes,
        in_specs=[anywhere] * (PARTS + len(blocks)) + [whole] * len(before),
        out_specs=(whole,) * len(shapes),
        scratch_shapes=score_scratch(SLAB, total, feats, len(blocks)),
        compiler_params=pltpu.CompilerParams(vmem_limit_bytes=24 * MEBIBYTE),
        cost_estimate=score_cost(SLAB, total, feats),
        name=name,
    )(*slab_parts, *blocks, *before)


def cut_kernel(chosen_ref, slab_ref, *refs, pieces, size):
    outs, sems = refs[-1 - len(pieces) : -1], refs[-1]
    copies = []
    for index, (j, begin, rows) in enumerate(pieces):
        start = pl.multiple_of(chosen_ref[0, j] * size + begin, 32)
        copies.append(pltpu.make_async_copy(slab_ref.at[pl.ds(start, rows)], outs[index], sems.at[index]))
        copies[-1].start()
    for copy in copies:
        copy.wait()


def cut(neighbours, slab_part, pieces, size, after):
    feats = slab_part.shape[1]
    anywhere = pl.BlockSpec(memory_space=pl.ANY)
    return pl.pallas_call(
        functools.partial(cut_kernel, pieces=pieces, size=size),
        out_shape=tuple(jax.ShapeDtypeStruct((rows, feats), slab_part.dtype) for _, _, rows in pieces),
        in_specs=[pl.BlockSpec(memory_space=pltpu.SMEM)] + [anywhere] * (1 + len(after)),
        out_specs=(anywhere,) * len(pieces),
        scratch_shapes=[pltpu.SemaphoreType.DMA((len(pieces),))],
        compiler_params=pltpu.CompilerParams(vmem_limit_bytes=MOST_VMEM if after else 2 * MEBIBYTE),
        cost_estimate=pl.CostEstimate(flops=0, bytes_accessed=8 * size * feats, transcendentals=0),
        name="cut",
    )(neighbours, slab_part, *after)


def answer_kernel(counts_ref, answers_ref, out_ref):
    counts_row = counts_ref[...].astype(jnp.float32)
    owners, capacity = answers_ref.shape
    docs = out_ref.shape[1]
    owner = lax.broadcasted_iota(jnp.int32, (owners, 1), 0)
    before, own = column_starts(counts_row, owner)
    position = lax.broadcasted_iota(jnp.int32, (owners, docs), 1).astype(jnp.float32)
    mine = (position >= before) & (position < before + own)
    start = jnp.sum(jnp.where(mine, before, 0.0), axis=0, keepdims=True)
    rank = (position[:1] - start).astype(jnp.int32)
    spread = lax.dot_general(
        answers_ref[...],
        jnp.where(mine, 1.0, 0.0),
        (((0,), (0,)), ((), ())),
        precision=lax.Precision.HIGHEST,
        preferred_element_type=jnp.float32,
    )
    ranks = lax.broadcasted_iota(jnp.int32, (capacity, docs), 0)
    found = jnp.sum(jnp.where(ranks == rank, spread, 0.0), axis=0, keepdims=True)
    out_ref[...] = found * (1.0 / 1024.0)


def passed_along(x, axis, by):
    length = lax.axis_size(axis)
    return lax.ppermute(x, axis, [(i, (i + by) % length) for i in range(length)])


def body(documents, counts, neighbours):
    dp_count = lax.axis_size("dp")
    pair_count = lax.axis_size("pair")
    row_count, feats = documents.shape
    capacity = SLAB // dp_count
    lanes = SLAB // BLOCK
    sources = dp_count // lanes
    chosen = neighbours[0]
    offsets = [1 + j % (pair_count - 1) for j in range(NEIGHBOURS)]

    sizes = [sources * width for width in WIDTHS]
    far = NEIGHBOURS - 1
    back = pair_count - offsets[far]

    def exchanged(part):
        return lax.all_to_all(part, "dp", split_axis=0, concat_axis=0, tiled=True)

    def sent_blocks(index, slab_part, after):
        size, relayed = sizes[index], RELAYED[index]
        pieces = [(far, 0, relayed)] + [(j, 0, size) for j in range(far)]
        if relayed < size:
            pieces.append((far, relayed, size - relayed))
        long_way, *outward = cut(neighbours, slab_part, pieces, size, after)
        half_way = passed_along(long_way, "pair", -(back - back // 2))
        near = [passed_along(outward[j], "pair", offsets[j]) for j in range(far)]
        direct = [passed_along(piece, "pair", offsets[far]) for piece in outward[far:]]
        return half_way, near, direct

    def rest_of_the_way(half_way):
        return passed_along(half_way, "pair", -(back // 2))

    outgoing = outgoing_parts(counts, documents)
    slab_0 = exchanged(outgoing[0])
    slab_1 = exchanged(outgoing[1])
    half_way, near_0, direct_0 = sent_blocks(0, slab_0, [])
    far_0 = [rest_of_the_way(half_way)] + direct_0
    arrived = sum(block[:16, :128] for block in [half_way] + near_0)
    half_way, near_1, direct_1 = sent_blocks(1, slab_1, [arrived])
    far_1 = [rest_of_the_way(half_way)] + direct_1

    slab_parts = [slab_0, slab_1]
    slab_best, blocks_0, row_bias = fold_blocks(slab_parts, near_0 + far_0, (), "early_scores")
    slab_best, blocks_1 = fold_blocks(slab_parts, near_1, (row_bias, slab_best), "near_scores")
    slab_best, far_best = fold_blocks(slab_parts, far_1, (row_bias, slab_best), "last_scores")
    blocks_1 = [blocks_1[:, j * sizes[1] : (j + 1) * sizes[1]] for j in range(far)] + [far_best]
    returned = [
        passed_along(
            jnp.concatenate([blocks_0[:, j * sizes[0] : (j + 1) * sizes[0]], blocks_1[j]], axis=1),
            "pair",
            -offsets[j],
        )
        for j in range(NEIGHBOURS)
    ]

    block_number = jnp.arange(lanes, dtype=jnp.int32)[:, None]
    pieces = []
    slot = 0
    for width, size in zip(WIDTHS, sizes):
        best = slab_best[0, slot * lanes : (slot + size) * lanes].reshape(lanes, size)
        for j in range(NEIGHBOURS):
            here = returned[j][:, slot : slot + size]
            best = jnp.maximum(best, jnp.where(block_number == chosen[j], here, FLOOR * 1024.0))
        pieces.append(best.reshape(dp_count, width))
        slot += size
    best = jnp.concatenate(pieces, axis=1)
    answers = lax.all_to_all(best, "dp", split_axis=0, concat_axis=0, tiled=True)
    found = pl.pallas_call(
        answer_kernel,
        out_shape=jax.ShapeDtypeStruct((1, row_count), jnp.float32),
        compiler_params=pltpu.CompilerParams(vmem_limit_bytes=24 * MEBIBYTE),
        name="answer",
    )(counts, answers)
    return found.reshape(row_count)


def solution(mesh):
    return jax.shard_map(
        body,
        mesh=mesh,
        in_specs=(P(("dp", "pair"), None), P(("dp", "pair"), None), P(("dp", "pair"), None)),
        out_specs=P(("dp", "pair")),
        check_vma=False,
    )
```

```python
import functools

import jax
import jax.numpy as jnp
from jax import lax
from jax.experimental import pallas as pl
from jax.experimental.pallas import tpu as pltpu
from jax.sharding import PartitionSpec as P

BLOCK = 512
NEIGHBOURS = 3
SLAB = 2048
WIDTHS = (16, 16)
RELAYED = (256, 176)
PARTS = len(WIDTHS)
CHUNK = 256
FLOOR = -2.0
DEAD = -1e9
MARK = 64.0
MEBIBYTE = 1024 * 1024
MOST_VMEM = 60 * MEBIBYTE

NT = (((1,), (1,)), ((), ()))


def column_starts(counts_row, owner_column):
    owners = lax.broadcasted_iota(jnp.int32, (owner_column.shape[0], counts_row.shape[1]), 1)
    before = jnp.sum(jnp.where(owners < owner_column, counts_row, 0.0), axis=1, keepdims=True)
    own = jnp.sum(jnp.where(owners == owner_column, counts_row, 0.0), axis=1, keepdims=True)
    return before, own


def picked_rows(counts_row, unit_ref, start, tile, first, width):
    slot = lax.broadcasted_iota(jnp.int32, (tile, 1), 0) + start
    owner = lax.shift_right_logical(slot, width.bit_length() - 1)
    rank = (lax.bitwise_and(slot, width - 1) + first).astype(jnp.float32)
    before, own = column_starts(counts_row, owner)
    live = rank < own
    wanted = jnp.where(live, before + rank, -1.0).astype(jnp.int32)
    lane = lax.broadcasted_iota(jnp.int32, (tile, unit_ref.shape[0]), 1)
    choice = jnp.where(lane == wanted, 1.0, 0.0).astype(jnp.bfloat16)
    picked = jnp.dot(choice, unit_ref[...], preferred_element_type=jnp.float32)
    place = lax.broadcasted_iota(jnp.int32, (tile, picked.shape[1]), 1)
    return jnp.where((place == 0) & (wanted < 0), MARK, picked).astype(jnp.bfloat16)


def first_kernel(counts_ref, documents_ref, unit_out, part_out, raw, unit, part, in_sem, unit_sem, part_sem, *, width):
    tile = 128
    steps = raw.shape[0] // tile
    loads = []
    for step in range(steps):
        here = pl.ds(step * tile, tile)
        loads.append(pltpu.make_async_copy(documents_ref.at[here], raw.at[here], in_sem.at[step]))
        loads[-1].start()
    for step in range(steps):
        here = pl.ds(step * tile, tile)
        loads[step].wait()
        values = raw[here, :].astype(jnp.float32)
        mean = jnp.mean(values * values, axis=-1, keepdims=True)
        unit[here, :] = (values * lax.rsqrt(mean + 1e-06)).astype(jnp.bfloat16)
    stores = [pltpu.make_async_copy(unit, unit_out, unit_sem)]
    stores[-1].start()
    counts_row = counts_ref[...].astype(jnp.float32)
    tile = 256
    for step in range(part.shape[0] // tile):
        here = pl.ds(step * tile, tile)
        part[here, :] = picked_rows(counts_row, unit, step * tile, tile, 0, width)
        stores.append(pltpu.make_async_copy(part.at[here], part_out.at[here], part_sem.at[step]))
        stores[-1].start()
    for store in stores:
        store.wait()


def later_kernel(counts_ref, unit_ref, out_ref, *, first, width):
    counts_row = counts_ref[...].astype(jnp.float32)
    tile = 256

    @pl.loop(0, out_ref.shape[0] // tile)
    def _(step):
        here = pl.ds(pl.multiple_of(step * tile, tile), tile)
        out_ref[here, :] = picked_rows(counts_row, unit_ref, step * tile, tile, first, width)


def outgoing_parts(counts, documents):
    owners = counts.shape[1]
    rows, feats = documents.shape
    width = WIDTHS[0]
    size = owners * width
    shape = lambda n: jax.ShapeDtypeStruct((n, feats), jnp.bfloat16)
    cost = lambda n: pl.CostEstimate(
        flops=2 * n * rows * feats, bytes_accessed=2 * (n + rows) * feats, transcendentals=0
    )
    whole = pl.BlockSpec(memory_space=pltpu.VMEM)
    anywhere = pl.BlockSpec(memory_space=pltpu.HBM)
    unit, part = pl.pallas_call(
        functools.partial(first_kernel, width=width),
        out_shape=(shape(rows), shape(size)),
        in_specs=[whole, anywhere],
        out_specs=(anywhere, anywhere),
        scratch_shapes=[
            pltpu.VMEM((rows, feats), jnp.bfloat16),
            pltpu.VMEM((rows, feats), jnp.bfloat16),
            pltpu.VMEM((size, feats), jnp.bfloat16),
            pltpu.SemaphoreType.DMA((rows // 128,)),
            pltpu.SemaphoreType.DMA,
            pltpu.SemaphoreType.DMA((size // 256,)),
        ],
        compiler_params=pltpu.CompilerParams(vmem_limit_bytes=MOST_VMEM),
        cost_estimate=cost(size),
        name="unit_and_pick",
    )(counts, documents)
    parts = [part]
    first = width
    for width in WIDTHS[1:]:
        parts.append(
            pl.pallas_call(
                functools.partial(later_kernel, first=first, width=width),
                out_shape=shape(owners * width),
                in_specs=[whole, whole],
                out_specs=whole,
                compiler_params=pltpu.CompilerParams(vmem_limit_bytes=24 * MEBIBYTE),
                cost_estimate=cost(owners * width),
                name="pick",
            )(counts, unit)
        )
        first += width
    return parts


def score_tile(scores, row_bias, column_bias, best_ref, rows):
    live = scores + row_bias
    part = best_ref[rows, :]
    for lane in range(0, scores.shape[1], 128):
        part = jnp.maximum(part, live[:, lane : lane + 128])
    best_ref[rows, :] = part
    return jnp.max(scores + column_bias, axis=0, keepdims=True)


def block_bias(block):
    return jnp.where(block[:, 0:1].astype(jnp.float32) > 0.75 * MARK, DEAD, 0.0)


def best_row(best_ref, rows):
    turned = best_ref[rows, :].T
    return jnp.max(turned, axis=0, keepdims=True)


def row_offsets(refs):
    offsets = [0]
    for ref in refs:
        offsets.append(offsets[-1] + ref.shape[0])
    return offsets


def loads_of(refs, target, sems):
    offsets = row_offsets(refs)
    return [
        pltpu.make_async_copy(ref, target.at[pl.ds(offset, ref.shape[0])], sems.at[i])
        for i, (ref, offset) in enumerate(zip(refs, offsets))
    ]


def fold_scores(slab_refs, blocks, best, row_bias_of, slab_best_of, slab_best_ref):
    tile = 256
    for slab_ref, offset in zip(slab_refs, row_offsets(slab_refs)):

        @pl.loop(0, slab_ref.shape[0] // tile)
        def _(step, slab_ref=slab_ref, offset=offset):
            there = pl.ds(pl.multiple_of(offset + step * tile, tile), tile)
            here = slab_ref[pl.ds(pl.multiple_of(step * tile, tile), tile), :]
            row_bias = row_bias_of(there, here)
            slab_best = slab_best_of(there)
            for begin in range(0, blocks.shape[0], CHUNK):
                rows = pl.ds(begin, CHUNK)
                block = blocks[rows, :]
                scores = lax.dot_general(block, here, NT, preferred_element_type=jnp.float32)
                slab_best = jnp.maximum(
                    slab_best, score_tile(scores, row_bias, block_bias(block), best, rows)
                )
            slab_best_ref[:, there] = slab_best

    return jnp.concatenate(
        [best_row(best, pl.ds(begin, CHUNK)) for begin in range(0, blocks.shape[0], CHUNK)], axis=1
    )


def score_kernel(*refs, count, first):
    slab_refs, block_refs = refs[:PARTS], refs[PARTS : PARTS + count]
    refs = refs[PARTS + count :]
    if first:
        slab_best_ref, block_best_ref, row_bias_ref, blocks, best, block_sem = refs
    else:
        row_bias_ref, before_ref, slab_best_ref, block_best_ref, blocks, best, block_sem = refs
    block_loads = loads_of(block_refs, blocks, block_sem)
    for load in block_loads:
        load.start()
    best[...] = jnp.full(best.shape, 4 * DEAD, jnp.float32)
    for load in block_loads:
        load.wait()

    def row_bias_of(there, here):
        if not first:
            return row_bias_ref[:, there]
        marks = here[:, 0:128].astype(jnp.float32).T[0:1, :]
        row_bias = jnp.where(marks > 0.75 * MARK, DEAD, 0.0)
        row_bias_ref[:, there] = row_bias
        return row_bias

    def slab_best_of(there):
        if not first:
            return before_ref[:, there]
        return jnp.full((1, there.size), FLOOR * 1024.0, jnp.float32)

    block_best_ref[...] = fold_scores(slab_refs, blocks, best, row_bias_of, slab_best_of, slab_best_ref)


def fold_blocks(slab_parts, blocks, before, name):
    feats = slab_parts[0].shape[1]
    whole = pl.BlockSpec(memory_space=pltpu.VMEM)
    anywhere = pl.BlockSpec(memory_space=pl.ANY)
    total = sum(block.shape[0] for block in blocks)
    row = lambda n: jax.ShapeDtypeStruct((1, n), jnp.float32)
    shapes = (row(SLAB), row(total)) if before else (row(SLAB), row(total), row(SLAB))
    return pl.pallas_call(
        functools.partial(score_kernel, count=len(blocks), first=not before),
        out_shape=shapes,
        in_specs=[whole] * PARTS + [anywhere] * len(blocks) + [whole] * len(before),
        out_specs=(whole,) * len(shapes),
        scratch_shapes=[
            pltpu.VMEM((total, feats), jnp.bfloat16),
            pltpu.VMEM((total, 128), jnp.float32),
            pltpu.SemaphoreType.DMA((len(blocks),)),
        ],
        compiler_params=pltpu.CompilerParams(vmem_limit_bytes=24 * MEBIBYTE),
        cost_estimate=pl.CostEstimate(
            flops=2 * SLAB * total * feats, bytes_accessed=2 * (SLAB + total) * feats, transcendentals=0
        ),
        name=name,
    )(*slab_parts, *blocks, *before)


def cut_kernel(chosen_ref, slab_ref, *refs, pieces, size):
    outs = refs[-3 - len(pieces) : -3]
    staged, load_sem, store_sem = refs[-3:]
    loads, stores = [], []
    offset = 0
    for index, (j, begin, rows) in enumerate(pieces):
        start = pl.multiple_of(chosen_ref[0, j] * size + begin, 16)
        stage = staged.at[pl.ds(offset, rows)]
        loads.append(pltpu.make_async_copy(slab_ref.at[pl.ds(start, rows)], stage, load_sem.at[index]))
        stores.append(pltpu.make_async_copy(stage, outs[index], store_sem.at[index]))
        loads[-1].start()
        offset += rows
    for load, store in zip(loads, stores):
        load.wait()
        store.start()
    for store in stores:
        store.wait()


def cut(neighbours, slab_part, pieces, size, after):
    feats = slab_part.shape[1]
    anywhere = pl.BlockSpec(memory_space=pl.ANY)
    return pl.pallas_call(
        functools.partial(cut_kernel, pieces=pieces, size=size),
        out_shape=tuple(jax.ShapeDtypeStruct((rows, feats), slab_part.dtype) for _, _, rows in pieces),
        in_specs=[pl.BlockSpec(memory_space=pltpu.SMEM)] + [anywhere] * (1 + len(after)),
        out_specs=(anywhere,) * len(pieces),
        scratch_shapes=[
            pltpu.VMEM((sum(rows for _, _, rows in pieces), feats), slab_part.dtype),
            pltpu.SemaphoreType.DMA((len(pieces),)),
            pltpu.SemaphoreType.DMA((len(pieces),)),
        ],
        compiler_params=pltpu.CompilerParams(vmem_limit_bytes=MOST_VMEM if after else 4 * MEBIBYTE),
        cost_estimate=pl.CostEstimate(flops=0, bytes_accessed=8 * size * feats, transcendentals=0),
        name="cut",
    )(neighbours, slab_part, *after)


def answer_kernel(counts_ref, answers_ref, out_ref):
    counts_row = counts_ref[...].astype(jnp.float32)
    owners, capacity = answers_ref.shape
    docs = out_ref.shape[1]
    owner = lax.broadcasted_iota(jnp.int32, (owners, 1), 0)
    before, own = column_starts(counts_row, owner)
    position = lax.broadcasted_iota(jnp.int32, (owners, docs), 1).astype(jnp.float32)
    mine = (position >= before) & (position < before + own)
    start = jnp.sum(jnp.where(mine, before, 0.0), axis=0, keepdims=True)
    rank = (position[:1] - start).astype(jnp.int32)
    spread = lax.dot_general(
        answers_ref[...],
        jnp.where(mine, 1.0, 0.0),
        (((0,), (0,)), ((), ())),
        precision=lax.Precision.HIGHEST,
        preferred_element_type=jnp.float32,
    )
    ranks = lax.broadcasted_iota(jnp.int32, (capacity, docs), 0)
    found = jnp.sum(jnp.where(ranks == rank, spread, 0.0), axis=0, keepdims=True)
    out_ref[...] = found * (1.0 / 1024.0)


def passed_along(x, axis, by):
    length = lax.axis_size(axis)
    return lax.ppermute(x, axis, [(i, (i + by) % length) for i in range(length)])


def body(documents, counts, neighbours):
    dp_count = lax.axis_size("dp")
    pair_count = lax.axis_size("pair")
    row_count, feats = documents.shape
    capacity = SLAB // dp_count
    lanes = SLAB // BLOCK
    sources = dp_count // lanes
    chosen = neighbours[0]
    offsets = [1 + j % (pair_count - 1) for j in range(NEIGHBOURS)]

    sizes = [sources * width for width in WIDTHS]
    far = NEIGHBOURS - 1
    back = pair_count - offsets[far]

    def exchanged(part):
        return lax.all_to_all(part, "dp", split_axis=0, concat_axis=0, tiled=True)

    def sent_blocks(index, slab_part, after):
        size, relayed = sizes[index], RELAYED[index]
        pieces = [(far, 0, relayed)] + [(j, 0, size) for j in range(far)]
        if relayed < size:
            pieces.append((far, relayed, size - relayed))
        long_way, *outward = cut(neighbours, slab_part, pieces, size, after)
        half_way = passed_along(long_way, "pair", -(back - back // 2))
        near = [passed_along(outward[j], "pair", offsets[j]) for j in range(far)]
        direct = [passed_along(piece, "pair", offsets[far]) for piece in outward[far:]]
        return half_way, near, direct

    def rest_of_the_way(half_way):
        return passed_along(half_way, "pair", -(back // 2))

    outgoing = outgoing_parts(counts, documents)
    slab_0 = exchanged(outgoing[0])
    slab_1 = exchanged(outgoing[1])
    half_way, near_0, direct_0 = sent_blocks(0, slab_0, [])
    far_0 = [rest_of_the_way(half_way)] + direct_0
    arrived = sum(block[:16, :128] for block in [half_way] + near_0)
    half_way, near_1, direct_1 = sent_blocks(1, slab_1, [arrived])
    far_1 = [rest_of_the_way(half_way)] + direct_1

    slab_parts = [slab_0, slab_1]
    slab_best, blocks_0, row_bias = fold_blocks(slab_parts, near_0 + far_0, (), "early_scores")
    slab_best, blocks_1 = fold_blocks(slab_parts, near_1, (row_bias, slab_best), "near_scores")
    slab_best, far_best = fold_blocks(slab_parts, far_1, (row_bias, slab_best), "last_scores")
    blocks_1 = [blocks_1[:, j * sizes[1] : (j + 1) * sizes[1]] for j in range(far)] + [far_best]
    returned = [
        passed_along(
            jnp.concatenate([blocks_0[:, j * sizes[0] : (j + 1) * sizes[0]], blocks_1[j]], axis=1),
            "pair",
            -offsets[j],
        )
        for j in range(NEIGHBOURS)
    ]

    block_number = jnp.arange(lanes, dtype=jnp.int32)[:, None]
    pieces = []
    slot = 0
    for width, size in zip(WIDTHS, sizes):
        best = slab_best[0, slot * lanes : (slot + size) * lanes].reshape(lanes, size)
        for j in range(NEIGHBOURS):
            here = returned[j][:, slot : slot + size]
            best = jnp.maximum(best, jnp.where(block_number == chosen[j], here, FLOOR * 1024.0))
        pieces.append(best.reshape(dp_count, width))
        slot += size
    best = jnp.concatenate(pieces, axis=1)
    answers = lax.all_to_all(best, "dp", split_axis=0, concat_axis=0, tiled=True)
    found = pl.pallas_call(
        answer_kernel,
        out_shape=jax.ShapeDtypeStruct((1, row_count), jnp.float32),
        compiler_params=pltpu.CompilerParams(vmem_limit_bytes=24 * MEBIBYTE),
        name="answer",
    )(counts, answers)
    return found.reshape(row_count)


def solution(mesh):
    return jax.shard_map(
        body,
        mesh=mesh,
        in_specs=(P(("dp", "pair"), None), P(("dp", "pair"), None), P(("dp", "pair"), None)),
        out_specs=P(("dp", "pair")),
        check_vma=False,
    )
```

```python
import functools

import jax
import jax.numpy as jnp
from jax import lax
from jax.experimental import pallas as pl
from jax.experimental.pallas import tpu as pltpu
from jax.sharding import PartitionSpec as P

BLOCK = 512
NEIGHBOURS = 3
SLAB = 2048
WIDTHS = (16, 16)
RELAYED = (256, 160)
PARTS = len(WIDTHS)
CHUNK = 256
FLOOR = -2.0
DEAD = -1e9
MARK = 64.0
MEBIBYTE = 1024 * 1024
MOST_VMEM = 60 * MEBIBYTE

NT = (((1,), (1,)), ((), ()))


def column_starts(counts_row, owner_column):
    owners = lax.broadcasted_iota(jnp.int32, (owner_column.shape[0], counts_row.shape[1]), 1)
    before = jnp.sum(jnp.where(owners < owner_column, counts_row, 0.0), axis=1, keepdims=True)
    own = jnp.sum(jnp.where(owners == owner_column, counts_row, 0.0), axis=1, keepdims=True)
    return before, own


def picked_rows(counts_row, unit_ref, start, tile, first, width):
    slot = lax.broadcasted_iota(jnp.int32, (tile, 1), 0) + start
    owner = lax.shift_right_logical(slot, width.bit_length() - 1)
    rank = (lax.bitwise_and(slot, width - 1) + first).astype(jnp.float32)
    before, own = column_starts(counts_row, owner)
    live = rank < own
    wanted = jnp.where(live, before + rank, -1.0).astype(jnp.int32)
    lane = lax.broadcasted_iota(jnp.int32, (tile, unit_ref.shape[0]), 1)
    choice = jnp.where(lane == wanted, 1.0, 0.0).astype(jnp.bfloat16)
    picked = jnp.dot(choice, unit_ref[...], preferred_element_type=jnp.float32)
    place = lax.broadcasted_iota(jnp.int32, (tile, picked.shape[1]), 1)
    return jnp.where((place == 0) & (wanted < 0), MARK, picked).astype(jnp.bfloat16)


def first_kernel(counts_ref, documents_ref, unit_out, part_out, raw, unit, part, in_sem, unit_sem, part_sem, *, width):
    tile = 128
    steps = raw.shape[0] // tile
    loads = []
    for step in range(steps):
        here = pl.ds(step * tile, tile)
        loads.append(pltpu.make_async_copy(documents_ref.at[here], raw.at[here], in_sem.at[step]))
        loads[-1].start()
    for step in range(steps):
        here = pl.ds(step * tile, tile)
        loads[step].wait()
        values = raw[here, :].astype(jnp.float32)
        mean = jnp.mean(values * values, axis=-1, keepdims=True)
        unit[here, :] = (values * lax.rsqrt(mean + 1e-06)).astype(jnp.bfloat16)
    stores = [pltpu.make_async_copy(unit, unit_out, unit_sem)]
    stores[-1].start()
    counts_row = counts_ref[...].astype(jnp.float32)
    tile = 256
    for step in range(part.shape[0] // tile):
        here = pl.ds(step * tile, tile)
        part[here, :] = picked_rows(counts_row, unit, step * tile, tile, 0, width)
        stores.append(pltpu.make_async_copy(part.at[here], part_out.at[here], part_sem.at[step]))
        stores[-1].start()
    for store in stores:
        store.wait()


def later_kernel(counts_ref, unit_ref, out_ref, *, first, width):
    counts_row = counts_ref[...].astype(jnp.float32)
    tile = 256

    @pl.loop(0, out_ref.shape[0] // tile)
    def _(step):
        here = pl.ds(pl.multiple_of(step * tile, tile), tile)
        out_ref[here, :] = picked_rows(counts_row, unit_ref, step * tile, tile, first, width)


def outgoing_parts(counts, documents):
    owners = counts.shape[1]
    rows, feats = documents.shape
    width = WIDTHS[0]
    size = owners * width
    shape = lambda n: jax.ShapeDtypeStruct((n, feats), jnp.bfloat16)
    cost = lambda n: pl.CostEstimate(
        flops=2 * n * rows * feats, bytes_accessed=2 * (n + rows) * feats, transcendentals=0
    )
    whole = pl.BlockSpec(memory_space=pltpu.VMEM)
    anywhere = pl.BlockSpec(memory_space=pltpu.HBM)
    unit, part = pl.pallas_call(
        functools.partial(first_kernel, width=width),
        out_shape=(shape(rows), shape(size)),
        in_specs=[whole, anywhere],
        out_specs=(anywhere, anywhere),
        scratch_shapes=[
            pltpu.VMEM((rows, feats), jnp.bfloat16),
            pltpu.VMEM((rows, feats), jnp.bfloat16),
            pltpu.VMEM((size, feats), jnp.bfloat16),
            pltpu.SemaphoreType.DMA((rows // 128,)),
            pltpu.SemaphoreType.DMA,
            pltpu.SemaphoreType.DMA((size // 256,)),
        ],
        compiler_params=pltpu.CompilerParams(vmem_limit_bytes=MOST_VMEM),
        cost_estimate=cost(size),
        name="unit_and_pick",
    )(counts, documents)
    parts = [part]
    first = width
    for width in WIDTHS[1:]:
        parts.append(
            pl.pallas_call(
                functools.partial(later_kernel, first=first, width=width),
                out_shape=shape(owners * width),
                in_specs=[whole, whole],
                out_specs=whole,
                compiler_params=pltpu.CompilerParams(vmem_limit_bytes=24 * MEBIBYTE),
                cost_estimate=cost(owners * width),
                name="pick",
            )(counts, unit)
        )
        first += width
    return parts


def score_tile(scores, row_bias, column_bias, best_ref, rows):
    live = scores + row_bias
    part = best_ref[rows, :]
    for lane in range(0, scores.shape[1], 128):
        part = jnp.maximum(part, live[:, lane : lane + 128])
    best_ref[rows, :] = part
    return jnp.max(scores + column_bias, axis=0, keepdims=True)


def block_bias(block):
    return jnp.where(block[:, 0:1].astype(jnp.float32) > 0.75 * MARK, DEAD, 0.0)


def best_row(best_ref, rows):
    turned = best_ref[rows, :].T
    return jnp.max(turned, axis=0, keepdims=True)


def row_offsets(refs):
    offsets = [0]
    for ref in refs:
        offsets.append(offsets[-1] + ref.shape[0])
    return offsets


def loads_of(refs, target, sems):
    offsets = row_offsets(refs)
    return [
        pltpu.make_async_copy(ref, target.at[pl.ds(offset, ref.shape[0])], sems.at[i])
        for i, (ref, offset) in enumerate(zip(refs, offsets))
    ]


TILE = 256


def tile_load(slab_ref, offset, step, slab, sems):
    rows = pl.ds(pl.multiple_of(step * TILE, TILE), TILE)
    there = pl.ds(pl.multiple_of(offset + step * TILE, TILE), TILE)
    return pltpu.make_async_copy(slab_ref.at[rows], slab.at[there], sems.at[offset // TILE + step])


def fold_scores(slab_refs, slab, slab_sem, blocks, best, row_bias_of, slab_best_of, slab_best_ref):
    for slab_ref, offset in zip(slab_refs, row_offsets(slab_refs)):

        @pl.loop(0, slab_ref.shape[0] // TILE)
        def _(step, slab_ref=slab_ref, offset=offset):
            tile_load(slab_ref, offset, step, slab, slab_sem).wait()
            there = pl.ds(pl.multiple_of(offset + step * TILE, TILE), TILE)
            here = slab[there, :]
            row_bias = row_bias_of(there, here)
            slab_best = slab_best_of(there)
            for begin in range(0, blocks.shape[0], CHUNK):
                rows = pl.ds(begin, CHUNK)
                block = blocks[rows, :]
                scores = lax.dot_general(block, here, NT, preferred_element_type=jnp.float32)
                slab_best = jnp.maximum(
                    slab_best, score_tile(scores, row_bias, block_bias(block), best, rows)
                )
            slab_best_ref[:, there] = slab_best

    return jnp.concatenate(
        [best_row(best, pl.ds(begin, CHUNK)) for begin in range(0, blocks.shape[0], CHUNK)], axis=1
    )


def score_kernel(*refs, count, first):
    slab_refs, block_refs = refs[:PARTS], refs[PARTS : PARTS + count]
    refs = refs[PARTS + count :]
    if first:
        slab_best_ref, block_best_ref, row_bias_ref, slab, blocks, best, slab_sem, block_sem = refs
    else:
        row_bias_ref, before_ref, slab_best_ref, block_best_ref, slab, blocks, best, slab_sem, block_sem = refs
    block_loads = loads_of(block_refs, blocks, block_sem)
    for load in block_loads:
        load.start()
    for slab_ref, offset in zip(slab_refs, row_offsets(slab_refs)):
        for step in range(slab_ref.shape[0] // TILE):
            tile_load(slab_ref, offset, step, slab, slab_sem).start()
    best[...] = jnp.full(best.shape, 4 * DEAD, jnp.float32)
    for load in block_loads:
        load.wait()

    def row_bias_of(there, here):
        if not first:
            return row_bias_ref[:, there]
        marks = here[:, 0:128].astype(jnp.float32).T[0:1, :]
        row_bias = jnp.where(marks > 0.75 * MARK, DEAD, 0.0)
        row_bias_ref[:, there] = row_bias
        return row_bias

    def slab_best_of(there):
        if not first:
            return before_ref[:, there]
        return jnp.full((1, there.size), FLOOR * 1024.0, jnp.float32)

    block_best_ref[...] = fold_scores(
        slab_refs, slab, slab_sem, blocks, best, row_bias_of, slab_best_of, slab_best_ref
    )


def fold_blocks(slab_parts, blocks, before, name):
    feats = slab_parts[0].shape[1]
    whole = pl.BlockSpec(memory_space=pltpu.VMEM)
    anywhere = pl.BlockSpec(memory_space=pl.ANY)
    total = sum(block.shape[0] for block in blocks)
    row = lambda n: jax.ShapeDtypeStruct((1, n), jnp.float32)
    shapes = (row(SLAB), row(total)) if before else (row(SLAB), row(total), row(SLAB))
    return pl.pallas_call(
        functools.partial(score_kernel, count=len(blocks), first=not before),
        out_shape=shapes,
        in_specs=[anywhere] * (PARTS + len(blocks)) + [whole] * len(before),
        out_specs=(whole,) * len(shapes),
        scratch_shapes=[
            pltpu.VMEM((SLAB, feats), jnp.bfloat16),
            pltpu.VMEM((total, feats), jnp.bfloat16),
            pltpu.VMEM((total, 128), jnp.float32),
            pltpu.SemaphoreType.DMA((SLAB // TILE,)),
            pltpu.SemaphoreType.DMA((len(blocks),)),
        ],
        compiler_params=pltpu.CompilerParams(vmem_limit_bytes=24 * MEBIBYTE),
        cost_estimate=pl.CostEstimate(
            flops=2 * SLAB * total * feats, bytes_accessed=2 * (SLAB + total) * feats, transcendentals=0
        ),
        name=name,
    )(*slab_parts, *blocks, *before)


def cut_kernel(chosen_ref, slab_ref, *refs, pieces, size):
    outs = refs[-3 - len(pieces) : -3]
    staged, load_sem, store_sem = refs[-3:]
    loads, stores = [], []
    offset = 0
    for index, (j, begin, rows) in enumerate(pieces):
        start = pl.multiple_of(chosen_ref[0, j] * size + begin, 16)
        stage = staged.at[pl.ds(offset, rows)]
        loads.append(pltpu.make_async_copy(slab_ref.at[pl.ds(start, rows)], stage, load_sem.at[index]))
        stores.append(pltpu.make_async_copy(stage, outs[index], store_sem.at[index]))
        loads[-1].start()
        offset += rows
    for load, store in zip(loads, stores):
        load.wait()
        store.start()
    for store in stores:
        store.wait()


def cut(neighbours, slab_part, pieces, size, after):
    feats = slab_part.shape[1]
    anywhere = pl.BlockSpec(memory_space=pl.ANY)
    return pl.pallas_call(
        functools.partial(cut_kernel, pieces=pieces, size=size),
        out_shape=tuple(jax.ShapeDtypeStruct((rows, feats), slab_part.dtype) for _, _, rows in pieces),
        in_specs=[pl.BlockSpec(memory_space=pltpu.SMEM)] + [anywhere] * (1 + len(after)),
        out_specs=(anywhere,) * len(pieces),
        scratch_shapes=[
            pltpu.VMEM((sum(rows for _, _, rows in pieces), feats), slab_part.dtype),
            pltpu.SemaphoreType.DMA((len(pieces),)),
            pltpu.SemaphoreType.DMA((len(pieces),)),
        ],
        compiler_params=pltpu.CompilerParams(vmem_limit_bytes=MOST_VMEM if after else 4 * MEBIBYTE),
        cost_estimate=pl.CostEstimate(flops=0, bytes_accessed=8 * size * feats, transcendentals=0),
        name="cut",
    )(neighbours, slab_part, *after)


def answer_kernel(counts_ref, answers_ref, out_ref):
    counts_row = counts_ref[...].astype(jnp.float32)
    owners, capacity = answers_ref.shape
    docs = out_ref.shape[1]
    owner = lax.broadcasted_iota(jnp.int32, (owners, 1), 0)
    before, own = column_starts(counts_row, owner)
    position = lax.broadcasted_iota(jnp.int32, (owners, docs), 1).astype(jnp.float32)
    mine = (position >= before) & (position < before + own)
    start = jnp.sum(jnp.where(mine, before, 0.0), axis=0, keepdims=True)
    rank = (position[:1] - start).astype(jnp.int32)
    spread = lax.dot_general(
        answers_ref[...],
        jnp.where(mine, 1.0, 0.0),
        (((0,), (0,)), ((), ())),
        precision=lax.Precision.HIGHEST,
        preferred_element_type=jnp.float32,
    )
    ranks = lax.broadcasted_iota(jnp.int32, (capacity, docs), 0)
    found = jnp.sum(jnp.where(ranks == rank, spread, 0.0), axis=0, keepdims=True)
    out_ref[...] = found * (1.0 / 1024.0)


def passed_along(x, axis, by):
    length = lax.axis_size(axis)
    return lax.ppermute(x, axis, [(i, (i + by) % length) for i in range(length)])


def body(documents, counts, neighbours):
    dp_count = lax.axis_size("dp")
    pair_count = lax.axis_size("pair")
    row_count, feats = documents.shape
    capacity = SLAB // dp_count
    lanes = SLAB // BLOCK
    sources = dp_count // lanes
    offsets = [1 + j % (pair_count - 1) for j in range(NEIGHBOURS)]

    sizes = [sources * width for width in WIDTHS]
    far = NEIGHBOURS - 1
    back = pair_count - offsets[far]

    def exchanged(part):
        return lax.all_to_all(part, "dp", split_axis=0, concat_axis=0, tiled=True)

    def sent_blocks(index, slab_part, after):
        size, relayed = sizes[index], RELAYED[index]
        pieces = [(far, 0, relayed)] + [(j, 0, size) for j in range(far)]
        if relayed < size:
            pieces.append((far, relayed, size - relayed))
        long_way, *outward = cut(neighbours, slab_part, pieces, size, after)
        half_way = passed_along(long_way, "pair", -(back - back // 2))
        near = [passed_along(outward[j], "pair", offsets[j]) for j in range(far)]
        direct = [passed_along(piece, "pair", offsets[far]) for piece in outward[far:]]
        return half_way, near, direct

    def rest_of_the_way(half_way):
        return passed_along(half_way, "pair", -(back // 2))

    outgoing = outgoing_parts(counts, documents)
    slab_0 = exchanged(outgoing[0])
    slab_1 = exchanged(outgoing[1])
    half_way, near_0, direct_0 = sent_blocks(0, slab_0, [])
    far_0 = [rest_of_the_way(half_way)] + direct_0
    arrived = sum(block[:16, :128] for block in [half_way] + near_0)
    half_way, near_1, direct_1 = sent_blocks(1, slab_1, [arrived])
    slab_parts = [slab_0, slab_1]
    slab_best, blocks_0, row_bias = fold_blocks(slab_parts, near_0 + far_0, (), "early_scores")
    half_way, blocks_0 = lax.optimization_barrier((half_way, blocks_0))
    far_1 = [rest_of_the_way(half_way)] + direct_1
    slab_best, blocks_1 = fold_blocks(slab_parts, near_1, (row_bias, slab_best), "near_scores")
    slab_best, far_best = fold_blocks(slab_parts, far_1, (row_bias, slab_best), "last_scores")
    blocks_1 = [blocks_1[:, j * sizes[1] : (j + 1) * sizes[1]] for j in range(far)] + [far_best]
    returned = [
        passed_along(
            jnp.concatenate([blocks_0[:, j * sizes[0] : (j + 1) * sizes[0]], blocks_1[j]], axis=1),
            "pair",
            -offsets[j],
        )
        for j in range(NEIGHBOURS)
    ]

    block_number = jnp.arange(lanes, dtype=jnp.int32)[:, None]
    pieces = []
    slot = 0
    for width, size in zip(WIDTHS, sizes):
        best = slab_best[0, slot * lanes : (slot + size) * lanes].reshape(lanes, size)
        for j in range(NEIGHBOURS):
            here = returned[j][:, slot : slot + size]
            listed = block_number == neighbours[:, j : j + 1]
            best = jnp.maximum(best, jnp.where(listed, here, FLOOR * 1024.0))
        pieces.append(best.reshape(dp_count, width))
        slot += size
    best = jnp.concatenate(pieces, axis=1)
    answers = lax.all_to_all(best, "dp", split_axis=0, concat_axis=0, tiled=True)
    found = pl.pallas_call(
        answer_kernel,
        out_shape=jax.ShapeDtypeStruct((1, row_count), jnp.float32),
        compiler_params=pltpu.CompilerParams(vmem_limit_bytes=24 * MEBIBYTE),
        name="answer",
    )(counts, answers)
    return found.reshape(row_count)


def solution(mesh):
    return jax.shard_map(
        body,
        mesh=mesh,
        in_specs=(P(("dp", "pair"), None), P(("dp", "pair"), None), P(("dp", "pair"), None)),
        out_specs=P(("dp", "pair")),
        check_vma=False,
    )
```

```python
import functools

import jax
import jax.numpy as jnp
from jax import lax
from jax.experimental import pallas as pl
from jax.experimental.pallas import tpu as pltpu
from jax.sharding import PartitionSpec as P

BLOCK = 512
NEIGHBOURS = 3
SLAB = 2048
WIDTHS = (16, 16)
RELAYED = (256, 144)
PARTS = len(WIDTHS)
CHUNK = 256
FLOOR = -2.0
DEAD = -1e9
MARK = 64.0
MEBIBYTE = 1024 * 1024
MOST_VMEM = 60 * MEBIBYTE

NT = (((1,), (1,)), ((), ()))


def column_starts(counts_row, owner_column):
    owners = lax.broadcasted_iota(jnp.int32, (owner_column.shape[0], counts_row.shape[1]), 1)
    before = jnp.sum(jnp.where(owners < owner_column, counts_row, 0.0), axis=1, keepdims=True)
    own = jnp.sum(jnp.where(owners == owner_column, counts_row, 0.0), axis=1, keepdims=True)
    return before, own


def picked_rows(counts_row, unit_ref, start, tile, first, width):
    slot = lax.broadcasted_iota(jnp.int32, (tile, 1), 0) + start
    owner = lax.shift_right_logical(slot, width.bit_length() - 1)
    rank = (lax.bitwise_and(slot, width - 1) + first).astype(jnp.float32)
    before, own = column_starts(counts_row, owner)
    live = rank < own
    wanted = jnp.where(live, before + rank, -1.0).astype(jnp.int32)
    lane = lax.broadcasted_iota(jnp.int32, (tile, unit_ref.shape[0]), 1)
    choice = jnp.where(lane == wanted, 1.0, 0.0).astype(jnp.bfloat16)
    picked = jnp.dot(choice, unit_ref[...], preferred_element_type=jnp.float32)
    place = lax.broadcasted_iota(jnp.int32, (tile, picked.shape[1]), 1)
    return jnp.where((place == 0) & (wanted < 0), MARK, picked).astype(jnp.bfloat16)


def first_kernel(counts_ref, documents_ref, unit_out, part_out, raw, unit, part, in_sem, unit_sem, part_sem, *, width):
    tile = 128
    steps = raw.shape[0] // tile
    loads = []
    for step in range(steps):
        here = pl.ds(step * tile, tile)
        loads.append(pltpu.make_async_copy(documents_ref.at[here], raw.at[here], in_sem.at[step]))
        loads[-1].start()
    for step in range(steps):
        here = pl.ds(step * tile, tile)
        loads[step].wait()
        values = raw[here, :].astype(jnp.float32)
        mean = jnp.mean(values * values, axis=-1, keepdims=True)
        unit[here, :] = (values * lax.rsqrt(mean + 1e-06)).astype(jnp.bfloat16)
    stores = [pltpu.make_async_copy(unit, unit_out, unit_sem)]
    stores[-1].start()
    counts_row = counts_ref[...].astype(jnp.float32)
    tile = 256
    for step in range(part.shape[0] // tile):
        here = pl.ds(step * tile, tile)
        part[here, :] = picked_rows(counts_row, unit, step * tile, tile, 0, width)
        stores.append(pltpu.make_async_copy(part.at[here], part_out.at[here], part_sem.at[step]))
        stores[-1].start()
    for store in stores:
        store.wait()


def later_kernel(counts_ref, unit_ref, out_ref, *, first, width):
    counts_row = counts_ref[...].astype(jnp.float32)
    tile = 256

    @pl.loop(0, out_ref.shape[0] // tile)
    def _(step):
        here = pl.ds(pl.multiple_of(step * tile, tile), tile)
        out_ref[here, :] = picked_rows(counts_row, unit_ref, step * tile, tile, first, width)


def outgoing_parts(counts, documents):
    owners = counts.shape[1]
    rows, feats = documents.shape
    width = WIDTHS[0]
    size = owners * width
    shape = lambda n: jax.ShapeDtypeStruct((n, feats), jnp.bfloat16)
    cost = lambda n: pl.CostEstimate(
        flops=2 * n * rows * feats, bytes_accessed=2 * (n + rows) * feats, transcendentals=0
    )
    whole = pl.BlockSpec(memory_space=pltpu.VMEM)
    anywhere = pl.BlockSpec(memory_space=pltpu.HBM)
    unit, part = pl.pallas_call(
        functools.partial(first_kernel, width=width),
        out_shape=(shape(rows), shape(size)),
        in_specs=[whole, anywhere],
        out_specs=(anywhere, anywhere),
        scratch_shapes=[
            pltpu.VMEM((rows, feats), jnp.bfloat16),
            pltpu.VMEM((rows, feats), jnp.bfloat16),
            pltpu.VMEM((size, feats), jnp.bfloat16),
            pltpu.SemaphoreType.DMA((rows // 128,)),
            pltpu.SemaphoreType.DMA,
            pltpu.SemaphoreType.DMA((size // 256,)),
        ],
        compiler_params=pltpu.CompilerParams(vmem_limit_bytes=MOST_VMEM),
        cost_estimate=cost(size),
        name="unit_and_pick",
    )(counts, documents)
    parts = [part]
    first = width
    for width in WIDTHS[1:]:
        parts.append(
            pl.pallas_call(
                functools.partial(later_kernel, first=first, width=width),
                out_shape=shape(owners * width),
                in_specs=[whole, whole],
                out_specs=whole,
                compiler_params=pltpu.CompilerParams(vmem_limit_bytes=24 * MEBIBYTE),
                cost_estimate=cost(owners * width),
                name="pick",
            )(counts, unit)
        )
        first += width
    return parts


def score_tile(scores, row_bias, column_bias, best_ref, rows):
    live = scores + row_bias
    part = best_ref[rows, :]
    for lane in range(0, scores.shape[1], 128):
        part = jnp.maximum(part, live[:, lane : lane + 128])
    best_ref[rows, :] = part
    return jnp.max(scores + column_bias, axis=0, keepdims=True)


def block_bias(block):
    return jnp.where(block[:, 0:1].astype(jnp.float32) > 0.75 * MARK, DEAD, 0.0)


def best_row(best_ref, rows):
    turned = best_ref[rows, :].T
    return jnp.max(turned, axis=0, keepdims=True)


def row_offsets(refs):
    offsets = [0]
    for ref in refs:
        offsets.append(offsets[-1] + ref.shape[0])
    return offsets


def loads_of(refs, target, sems):
    offsets = row_offsets(refs)
    return [
        pltpu.make_async_copy(ref, target.at[pl.ds(offset, ref.shape[0])], sems.at[i])
        for i, (ref, offset) in enumerate(zip(refs, offsets))
    ]


TILE = 256


def tile_load(slab_ref, offset, step, slab, sems):
    rows = pl.ds(pl.multiple_of(step * TILE, TILE), TILE)
    there = pl.ds(pl.multiple_of(offset + step * TILE, TILE), TILE)
    return pltpu.make_async_copy(slab_ref.at[rows], slab.at[there], sems.at[offset // TILE + step])


def fold_scores(slab_refs, slab, slab_sem, blocks, best, row_bias_of, slab_best_of, slab_best_ref):
    for slab_ref, offset in zip(slab_refs, row_offsets(slab_refs)):

        @pl.loop(0, slab_ref.shape[0] // TILE)
        def _(step, slab_ref=slab_ref, offset=offset):
            tile_load(slab_ref, offset, step, slab, slab_sem).wait()
            there = pl.ds(pl.multiple_of(offset + step * TILE, TILE), TILE)
            here = slab[there, :]
            row_bias = row_bias_of(there, here)
            slab_best = slab_best_of(there)
            for begin in range(0, blocks.shape[0], CHUNK):
                rows = pl.ds(begin, CHUNK)
                block = blocks[rows, :]
                scores = lax.dot_general(block, here, NT, preferred_element_type=jnp.float32)
                slab_best = jnp.maximum(
                    slab_best, score_tile(scores, row_bias, block_bias(block), best, rows)
                )
            slab_best_ref[:, there] = slab_best

    return jnp.concatenate(
        [best_row(best, pl.ds(begin, CHUNK)) for begin in range(0, blocks.shape[0], CHUNK)], axis=1
    )


def score_kernel(*refs, count, first):
    slab_refs, block_refs = refs[:PARTS], refs[PARTS : PARTS + count]
    refs = refs[PARTS + count :]
    if first:
        slab_best_ref, block_best_ref, row_bias_ref, slab, blocks, best, slab_sem, block_sem = refs
    else:
        row_bias_ref, before_ref, slab_best_ref, block_best_ref, slab, blocks, best, slab_sem, block_sem = refs
    block_loads = loads_of(block_refs, blocks, block_sem)
    for load in block_loads:
        load.start()
    for slab_ref, offset in zip(slab_refs, row_offsets(slab_refs)):
        for step in range(slab_ref.shape[0] // TILE):
            tile_load(slab_ref, offset, step, slab, slab_sem).start()
    best[...] = jnp.full(best.shape, 4 * DEAD, jnp.float32)
    for load in block_loads:
        load.wait()

    def row_bias_of(there, here):
        if not first:
            return row_bias_ref[:, there]
        marks = here[:, 0:128].astype(jnp.float32).T[0:1, :]
        row_bias = jnp.where(marks > 0.75 * MARK, DEAD, 0.0)
        row_bias_ref[:, there] = row_bias
        return row_bias

    def slab_best_of(there):
        if not first:
            return before_ref[:, there]
        return jnp.full((1, there.size), FLOOR * 1024.0, jnp.float32)

    block_best_ref[...] = fold_scores(
        slab_refs, slab, slab_sem, blocks, best, row_bias_of, slab_best_of, slab_best_ref
    )


def fold_blocks(slab_parts, blocks, before, name):
    feats = slab_parts[0].shape[1]
    whole = pl.BlockSpec(memory_space=pltpu.VMEM)
    anywhere = pl.BlockSpec(memory_space=pl.ANY)
    total = sum(block.shape[0] for block in blocks)
    row = lambda n: jax.ShapeDtypeStruct((1, n), jnp.float32)
    shapes = (row(SLAB), row(total)) if before else (row(SLAB), row(total), row(SLAB))
    return pl.pallas_call(
        functools.partial(score_kernel, count=len(blocks), first=not before),
        out_shape=shapes,
        in_specs=[anywhere] * (PARTS + len(blocks)) + [whole] * len(before),
        out_specs=(whole,) * len(shapes),
        scratch_shapes=[
            pltpu.VMEM((SLAB, feats), jnp.bfloat16),
            pltpu.VMEM((total, feats), jnp.bfloat16),
            pltpu.VMEM((total, 128), jnp.float32),
            pltpu.SemaphoreType.DMA((SLAB // TILE,)),
            pltpu.SemaphoreType.DMA((len(blocks),)),
        ],
        compiler_params=pltpu.CompilerParams(vmem_limit_bytes=24 * MEBIBYTE),
        cost_estimate=pl.CostEstimate(
            flops=2 * SLAB * total * feats, bytes_accessed=2 * (SLAB + total) * feats, transcendentals=0
        ),
        name=name,
    )(*slab_parts, *blocks, *before)


def cut_kernel(chosen_ref, slab_ref, *refs, pieces, size):
    outs = refs[-3 - len(pieces) : -3]
    staged, load_sem, store_sem = refs[-3:]
    loads, stores = [], []
    offset = 0
    for index, (j, begin, rows) in enumerate(pieces):
        start = pl.multiple_of(chosen_ref[0, j] * size + begin, 16)
        stage = staged.at[pl.ds(offset, rows)]
        loads.append(pltpu.make_async_copy(slab_ref.at[pl.ds(start, rows)], stage, load_sem.at[index]))
        stores.append(pltpu.make_async_copy(stage, outs[index], store_sem.at[index]))
        loads[-1].start()
        offset += rows
    for load, store in zip(loads, stores):
        load.wait()
        store.start()
    for store in stores:
        store.wait()


def cut(neighbours, slab_part, pieces, size, after):
    feats = slab_part.shape[1]
    anywhere = pl.BlockSpec(memory_space=pl.ANY)
    return pl.pallas_call(
        functools.partial(cut_kernel, pieces=pieces, size=size),
        out_shape=tuple(jax.ShapeDtypeStruct((rows, feats), slab_part.dtype) for _, _, rows in pieces),
        in_specs=[pl.BlockSpec(memory_space=pltpu.SMEM)] + [anywhere] * (1 + len(after)),
        out_specs=(anywhere,) * len(pieces),
        scratch_shapes=[
            pltpu.VMEM((sum(rows for _, _, rows in pieces), feats), slab_part.dtype),
            pltpu.SemaphoreType.DMA((len(pieces),)),
            pltpu.SemaphoreType.DMA((len(pieces),)),
        ],
        compiler_params=pltpu.CompilerParams(vmem_limit_bytes=MOST_VMEM if after else 4 * MEBIBYTE),
        cost_estimate=pl.CostEstimate(flops=0, bytes_accessed=8 * size * feats, transcendentals=0),
        name="cut",
    )(neighbours, slab_part, *after)


def answer_kernel(counts_ref, answers_ref, out_ref):
    counts_row = counts_ref[...].astype(jnp.float32)
    owners, capacity = answers_ref.shape
    docs = out_ref.shape[1]
    owner = lax.broadcasted_iota(jnp.int32, (owners, 1), 0)
    before, own = column_starts(counts_row, owner)
    position = lax.broadcasted_iota(jnp.int32, (owners, docs), 1).astype(jnp.float32)
    mine = (position >= before) & (position < before + own)
    start = jnp.sum(jnp.where(mine, before, 0.0), axis=0, keepdims=True)
    rank = (position[:1] - start).astype(jnp.int32)
    spread = lax.dot_general(
        answers_ref[...],
        jnp.where(mine, 1.0, 0.0),
        (((0,), (0,)), ((), ())),
        precision=lax.Precision.HIGHEST,
        preferred_element_type=jnp.float32,
    )
    ranks = lax.broadcasted_iota(jnp.int32, (capacity, docs), 0)
    found = jnp.sum(jnp.where(ranks == rank, spread, 0.0), axis=0, keepdims=True)
    out_ref[...] = found * (1.0 / 1024.0)


def passed_along(x, axis, by):
    length = lax.axis_size(axis)
    return lax.ppermute(x, axis, [(i, (i + by) % length) for i in range(length)])


def body(documents, counts, neighbours):
    dp_count = lax.axis_size("dp")
    pair_count = lax.axis_size("pair")
    row_count, feats = documents.shape
    capacity = SLAB // dp_count
    lanes = SLAB // BLOCK
    sources = dp_count // lanes
    offsets = [1 + j % (pair_count - 1) for j in range(NEIGHBOURS)]

    sizes = [sources * width for width in WIDTHS]
    far = NEIGHBOURS - 1
    back = pair_count - offsets[far]

    def exchanged(part):
        return lax.all_to_all(part, "dp", split_axis=0, concat_axis=0, tiled=True)

    def pieces_of(index):
        size, relayed = sizes[index], RELAYED[index]
        others = [(j, 0, size) for j in range(far)]
        if relayed < size:
            others.append((far, relayed, size - relayed))
        return [(far, 0, relayed)], others

    def half_the_way(piece):
        return passed_along(piece, "pair", -(back - back // 2))

    def sent(pieces):
        moved = [passed_along(piece, "pair", offsets[min(j, far)]) for j, piece in enumerate(pieces)]
        return moved[:far], moved[far:]

    def rest_of_the_way(half_way):
        return passed_along(half_way, "pair", -(back // 2))

    outgoing = outgoing_parts(counts, documents)
    slab_0 = exchanged(outgoing[0])
    slab_1 = exchanged(outgoing[1])
    long_way, others = pieces_of(0)
    long_way, *others = cut(neighbours, slab_0, long_way + others, sizes[0], [])
    half_way = half_the_way(long_way)
    near_0, direct_0 = sent(others)
    far_0 = [rest_of_the_way(half_way)] + direct_0
    arrived = sum(block[:16, :128] for block in [half_way] + near_0)
    long_way, others = pieces_of(1)
    long_way, *others = cut(neighbours, slab_1, long_way + others, sizes[1], [arrived])
    near_1, direct_1 = sent(others)
    long_way, far_0[0] = lax.optimization_barrier((long_way, far_0[0]))
    half_way = half_the_way(long_way)
    slab_parts = [slab_0, slab_1]
    slab_best, blocks_0, row_bias = fold_blocks(slab_parts, near_0 + far_0, (), "early_scores")
    *near_1, _ = lax.optimization_barrier((*near_1, half_way))
    half_way, blocks_0 = lax.optimization_barrier((half_way, blocks_0))
    far_1 = [rest_of_the_way(half_way)] + direct_1
    slab_best, blocks_1 = fold_blocks(slab_parts, near_1, (row_bias, slab_best), "near_scores")
    slab_best, far_best = fold_blocks(slab_parts, far_1, (row_bias, slab_best), "last_scores")
    blocks_1 = [blocks_1[:, j * sizes[1] : (j + 1) * sizes[1]] for j in range(far)] + [far_best]
    returned = [
        passed_along(
            jnp.concatenate([blocks_0[:, j * sizes[0] : (j + 1) * sizes[0]], blocks_1[j]], axis=1),
            "pair",
            -offsets[j],
        )
        for j in range(NEIGHBOURS)
    ]

    block_number = jnp.arange(lanes, dtype=jnp.int32)[:, None]
    pieces = []
    slot = 0
    for width, size in zip(WIDTHS, sizes):
        best = slab_best[0, slot * lanes : (slot + size) * lanes].reshape(lanes, size)
        for j in range(NEIGHBOURS):
            here = returned[j][:, slot : slot + size]
            listed = block_number == neighbours[:, j : j + 1]
            best = jnp.maximum(best, jnp.where(listed, here, FLOOR * 1024.0))
        pieces.append(best.reshape(dp_count, width))
        slot += size
    best = jnp.concatenate(pieces, axis=1)
    answers = lax.all_to_all(best, "dp", split_axis=0, concat_axis=0, tiled=True)
    found = pl.pallas_call(
        answer_kernel,
        out_shape=jax.ShapeDtypeStruct((1, row_count), jnp.float32),
        compiler_params=pltpu.CompilerParams(vmem_limit_bytes=24 * MEBIBYTE),
        name="answer",
    )(counts, answers)
    return found.reshape(row_count)


def solution(mesh):
    return jax.shard_map(
        body,
        mesh=mesh,
        in_specs=(P(("dp", "pair"), None), P(("dp", "pair"), None), P(("dp", "pair"), None)),
        out_specs=P(("dp", "pair")),
        check_vma=False,
    )
```

```python
import functools

import jax
import jax.numpy as jnp
from jax import lax
from jax.experimental import pallas as pl
from jax.experimental.pallas import tpu as pltpu
from jax.sharding import PartitionSpec as P

BLOCK = 512
NEIGHBOURS = 3
SLAB = 2048
WIDTHS = (16, 16)
RELAYED = (256, 128)
PARTS = len(WIDTHS)
CHUNK = 256
FLOOR = -2.0
DEAD = -1e9
MARK = 64.0
MEBIBYTE = 1024 * 1024
MOST_VMEM = 60 * MEBIBYTE

NT = (((1,), (1,)), ((), ()))


def column_starts(counts_row, owner_column):
    owners = lax.broadcasted_iota(jnp.int32, (owner_column.shape[0], counts_row.shape[1]), 1)
    before = jnp.sum(jnp.where(owners < owner_column, counts_row, 0.0), axis=1, keepdims=True)
    own = jnp.sum(jnp.where(owners == owner_column, counts_row, 0.0), axis=1, keepdims=True)
    return before, own


def picked_rows(counts_row, unit_ref, start, tile, first, width):
    slot = lax.broadcasted_iota(jnp.int32, (tile, 1), 0) + start
    owner = lax.shift_right_logical(slot, width.bit_length() - 1)
    rank = (lax.bitwise_and(slot, width - 1) + first).astype(jnp.float32)
    before, own = column_starts(counts_row, owner)
    live = rank < own
    wanted = jnp.where(live, before + rank, -1.0).astype(jnp.int32)
    lane = lax.broadcasted_iota(jnp.int32, (tile, unit_ref.shape[0]), 1)
    choice = jnp.where(lane == wanted, 1.0, 0.0).astype(jnp.bfloat16)
    picked = jnp.dot(choice, unit_ref[...], preferred_element_type=jnp.float32)
    place = lax.broadcasted_iota(jnp.int32, (tile, picked.shape[1]), 1)
    return jnp.where((place == 0) & (wanted < 0), MARK, picked).astype(jnp.bfloat16)


def first_kernel(counts_ref, documents_ref, unit_out, part_out, raw, unit, part, in_sem, unit_sem, part_sem, *, width):
    tile = 128
    steps = raw.shape[0] // tile
    loads = []
    for step in range(steps):
        here = pl.ds(step * tile, tile)
        loads.append(pltpu.make_async_copy(documents_ref.at[here], raw.at[here], in_sem.at[step]))
        loads[-1].start()
    for step in range(steps):
        here = pl.ds(step * tile, tile)
        loads[step].wait()
        values = raw[here, :].astype(jnp.float32)
        mean = jnp.mean(values * values, axis=-1, keepdims=True)
        unit[here, :] = (values * lax.rsqrt(mean + 1e-06)).astype(jnp.bfloat16)
    stores = [pltpu.make_async_copy(unit, unit_out, unit_sem)]
    stores[-1].start()
    counts_row = counts_ref[...].astype(jnp.float32)
    tile = 256
    for step in range(part.shape[0] // tile):
        here = pl.ds(step * tile, tile)
        part[here, :] = picked_rows(counts_row, unit, step * tile, tile, 0, width)
        stores.append(pltpu.make_async_copy(part.at[here], part_out.at[here], part_sem.at[step]))
        stores[-1].start()
    for store in stores:
        store.wait()


def later_kernel(counts_ref, unit_ref, out_ref, *, first, width):
    counts_row = counts_ref[...].astype(jnp.float32)
    tile = 256

    @pl.loop(0, out_ref.shape[0] // tile)
    def _(step):
        here = pl.ds(pl.multiple_of(step * tile, tile), tile)
        out_ref[here, :] = picked_rows(counts_row, unit_ref, step * tile, tile, first, width)


def outgoing_parts(counts, documents):
    owners = counts.shape[1]
    rows, feats = documents.shape
    width = WIDTHS[0]
    size = owners * width
    shape = lambda n: jax.ShapeDtypeStruct((n, feats), jnp.bfloat16)
    cost = lambda n: pl.CostEstimate(
        flops=2 * n * rows * feats, bytes_accessed=2 * (n + rows) * feats, transcendentals=0
    )
    whole = pl.BlockSpec(memory_space=pltpu.VMEM)
    anywhere = pl.BlockSpec(memory_space=pltpu.HBM)
    unit, part = pl.pallas_call(
        functools.partial(first_kernel, width=width),
        out_shape=(shape(rows), shape(size)),
        in_specs=[whole, anywhere],
        out_specs=(anywhere, anywhere),
        scratch_shapes=[
            pltpu.VMEM((rows, feats), jnp.bfloat16),
            pltpu.VMEM((rows, feats), jnp.bfloat16),
            pltpu.VMEM((size, feats), jnp.bfloat16),
            pltpu.SemaphoreType.DMA((rows // 128,)),
            pltpu.SemaphoreType.DMA,
            pltpu.SemaphoreType.DMA((size // 256,)),
        ],
        compiler_params=pltpu.CompilerParams(vmem_limit_bytes=MOST_VMEM),
        cost_estimate=cost(size),
        name="unit_and_pick",
    )(counts, documents)
    parts = [part]
    first = width
    for width in WIDTHS[1:]:
        parts.append(
            pl.pallas_call(
                functools.partial(later_kernel, first=first, width=width),
                out_shape=shape(owners * width),
                in_specs=[whole, whole],
                out_specs=whole,
                compiler_params=pltpu.CompilerParams(vmem_limit_bytes=24 * MEBIBYTE),
                cost_estimate=cost(owners * width),
                name="pick",
            )(counts, unit)
        )
        first += width
    return parts


def score_tile(scores, row_bias, column_bias, best_ref, rows):
    live = scores + row_bias
    part = best_ref[rows, :]
    for lane in range(0, scores.shape[1], 128):
        part = jnp.maximum(part, live[:, lane : lane + 128])
    best_ref[rows, :] = part
    return jnp.max(scores + column_bias, axis=0, keepdims=True)


def block_bias(block):
    return jnp.where(block[:, 0:1].astype(jnp.float32) > 0.75 * MARK, DEAD, 0.0)


def best_row(best_ref, rows):
    turned = best_ref[rows, :].T
    return jnp.max(turned, axis=0, keepdims=True)


def row_offsets(refs):
    offsets = [0]
    for ref in refs:
        offsets.append(offsets[-1] + ref.shape[0])
    return offsets


def loads_of(refs, target, sems):
    offsets = row_offsets(refs)
    return [
        pltpu.make_async_copy(ref, target.at[pl.ds(offset, ref.shape[0])], sems.at[i])
        for i, (ref, offset) in enumerate(zip(refs, offsets))
    ]


TILE = 256


def tile_load(slab_ref, offset, step, slab, sems):
    rows = pl.ds(pl.multiple_of(step * TILE, TILE), TILE)
    there = pl.ds(pl.multiple_of(offset + step * TILE, TILE), TILE)
    return pltpu.make_async_copy(slab_ref.at[rows], slab.at[there], sems.at[offset // TILE + step])


def fold_scores(slab_refs, slab, slab_sem, blocks, best, row_bias_of, slab_best_of, slab_best_ref):
    for slab_ref, offset in zip(slab_refs, row_offsets(slab_refs)):

        @pl.loop(0, slab_ref.shape[0] // TILE)
        def _(step, slab_ref=slab_ref, offset=offset):
            tile_load(slab_ref, offset, step, slab, slab_sem).wait()
            there = pl.ds(pl.multiple_of(offset + step * TILE, TILE), TILE)
            here = slab[there, :]
            row_bias = row_bias_of(there, here)
            slab_best = slab_best_of(there)
            for begin in range(0, blocks.shape[0], CHUNK):
                rows = pl.ds(begin, CHUNK)
                block = blocks[rows, :]
                scores = lax.dot_general(block, here, NT, preferred_element_type=jnp.float32)
                slab_best = jnp.maximum(
                    slab_best, score_tile(scores, row_bias, block_bias(block), best, rows)
                )
            slab_best_ref[:, there] = slab_best

    return jnp.concatenate(
        [best_row(best, pl.ds(begin, CHUNK)) for begin in range(0, blocks.shape[0], CHUNK)], axis=1
    )


def score_kernel(*refs, count, first):
    slab_refs, block_refs = refs[:PARTS], refs[PARTS : PARTS + count]
    refs = refs[PARTS + count :]
    if first:
        slab_best_ref, block_best_ref, row_bias_ref, slab, blocks, best, slab_sem, block_sem = refs
    else:
        row_bias_ref, before_ref, slab_best_ref, block_best_ref, slab, blocks, best, slab_sem, block_sem = refs
    block_loads = loads_of(block_refs, blocks, block_sem)
    for load in block_loads:
        load.start()
    for slab_ref, offset in zip(slab_refs, row_offsets(slab_refs)):
        for step in range(slab_ref.shape[0] // TILE):
            tile_load(slab_ref, offset, step, slab, slab_sem).start()
    best[...] = jnp.full(best.shape, 4 * DEAD, jnp.float32)
    for load in block_loads:
        load.wait()

    def row_bias_of(there, here):
        if not first:
            return row_bias_ref[:, there]
        marks = here[:, 0:128].astype(jnp.float32).T[0:1, :]
        row_bias = jnp.where(marks > 0.75 * MARK, DEAD, 0.0)
        row_bias_ref[:, there] = row_bias
        return row_bias

    def slab_best_of(there):
        if not first:
            return before_ref[:, there]
        return jnp.full((1, there.size), FLOOR * 1024.0, jnp.float32)

    block_best_ref[...] = fold_scores(
        slab_refs, slab, slab_sem, blocks, best, row_bias_of, slab_best_of, slab_best_ref
    )


def fold_blocks(slab_parts, blocks, before, name):
    feats = slab_parts[0].shape[1]
    whole = pl.BlockSpec(memory_space=pltpu.VMEM)
    anywhere = pl.BlockSpec(memory_space=pl.ANY)
    total = sum(block.shape[0] for block in blocks)
    row = lambda n: jax.ShapeDtypeStruct((1, n), jnp.float32)
    shapes = (row(SLAB), row(total)) if before else (row(SLAB), row(total), row(SLAB))
    return pl.pallas_call(
        functools.partial(score_kernel, count=len(blocks), first=not before),
        out_shape=shapes,
        in_specs=[anywhere] * (PARTS + len(blocks)) + [whole] * len(before),
        out_specs=(whole,) * len(shapes),
        scratch_shapes=[
            pltpu.VMEM((SLAB, feats), jnp.bfloat16),
            pltpu.VMEM((total, feats), jnp.bfloat16),
            pltpu.VMEM((total, 128), jnp.float32),
            pltpu.SemaphoreType.DMA((SLAB // TILE,)),
            pltpu.SemaphoreType.DMA((len(blocks),)),
        ],
        compiler_params=pltpu.CompilerParams(vmem_limit_bytes=24 * MEBIBYTE),
        cost_estimate=pl.CostEstimate(
            flops=2 * SLAB * total * feats, bytes_accessed=2 * (SLAB + total) * feats, transcendentals=0
        ),
        name=name,
    )(*slab_parts, *blocks, *before)


def cut_kernel(chosen_ref, slab_ref, *refs, pieces, size):
    outs, sems = refs[: len(pieces)], refs[-1]
    copies = []
    for index, (j, begin, rows) in enumerate(pieces):
        start = pl.multiple_of(chosen_ref[0, j] * size + begin, 16)
        copies.append(pltpu.make_async_copy(slab_ref.at[pl.ds(start, rows)], outs[index], sems.at[index]))
        copies[-1].start()
    for copy in copies:
        copy.wait()


def staged_cut_kernel(chosen_ref, slab_ref, *refs, pieces, size):
    outs = refs[-3 - len(pieces) : -3]
    staged, load_sem, store_sem = refs[-3:]
    loads, stores = [], []
    offset = 0
    for index, (j, begin, rows) in enumerate(pieces):
        start = pl.multiple_of(chosen_ref[0, j] * size + begin, 16)
        stage = staged.at[pl.ds(offset, rows)]
        loads.append(pltpu.make_async_copy(slab_ref.at[pl.ds(start, rows)], stage, load_sem.at[index]))
        stores.append(pltpu.make_async_copy(stage, outs[index], store_sem.at[index]))
        loads[-1].start()
        offset += rows
    for load, store in zip(loads, stores):
        load.wait()
        store.start()
    for store in stores:
        store.wait()


def cut(neighbours, slab_part, pieces, size, after):
    feats = slab_part.shape[1]
    anywhere = pl.BlockSpec(memory_space=pl.ANY)
    sems = pltpu.SemaphoreType.DMA((len(pieces),))
    stage = pltpu.VMEM((sum(rows for _, _, rows in pieces), feats), slab_part.dtype)
    kernel = staged_cut_kernel if after else cut_kernel
    return pl.pallas_call(
        functools.partial(kernel, pieces=pieces, size=size),
        out_shape=tuple(jax.ShapeDtypeStruct((rows, feats), slab_part.dtype) for _, _, rows in pieces),
        in_specs=[pl.BlockSpec(memory_space=pltpu.SMEM)] + [anywhere] * (1 + len(after)),
        out_specs=(anywhere,) * len(pieces),
        scratch_shapes=[stage, sems, sems] if after else [sems],
        compiler_params=pltpu.CompilerParams(vmem_limit_bytes=MOST_VMEM if after else 4 * MEBIBYTE),
        cost_estimate=pl.CostEstimate(flops=0, bytes_accessed=8 * size * feats, transcendentals=0),
        name="cut",
    )(neighbours, slab_part, *after)


def answer_kernel(counts_ref, answers_ref, out_ref):
    counts_row = counts_ref[...].astype(jnp.float32)
    owners, capacity = answers_ref.shape
    docs = out_ref.shape[1]
    owner = lax.broadcasted_iota(jnp.int32, (owners, 1), 0)
    before, own = column_starts(counts_row, owner)
    position = lax.broadcasted_iota(jnp.int32, (owners, docs), 1).astype(jnp.float32)
    mine = (position >= before) & (position < before + own)
    start = jnp.sum(jnp.where(mine, before, 0.0), axis=0, keepdims=True)
    rank = (position[:1] - start).astype(jnp.int32)
    spread = lax.dot_general(
        answers_ref[...],
        jnp.where(mine, 1.0, 0.0),
        (((0,), (0,)), ((), ())),
        precision=lax.Precision.HIGHEST,
        preferred_element_type=jnp.float32,
    )
    ranks = lax.broadcasted_iota(jnp.int32, (capacity, docs), 0)
    found = jnp.sum(jnp.where(ranks == rank, spread, 0.0), axis=0, keepdims=True)
    out_ref[...] = found * (1.0 / 1024.0)


def passed_along(x, axis, by):
    length = lax.axis_size(axis)
    return lax.ppermute(x, axis, [(i, (i + by) % length) for i in range(length)])


def body(documents, counts, neighbours):
    dp_count = lax.axis_size("dp")
    pair_count = lax.axis_size("pair")
    row_count, feats = documents.shape
    capacity = SLAB // dp_count
    lanes = SLAB // BLOCK
    sources = dp_count // lanes
    offsets = [1 + j % (pair_count - 1) for j in range(NEIGHBOURS)]

    sizes = [sources * width for width in WIDTHS]
    far = NEIGHBOURS - 1
    back = pair_count - offsets[far]

    def exchanged(part):
        return lax.all_to_all(part, "dp", split_axis=0, concat_axis=0, tiled=True)

    def pieces_of(index):
        size, relayed = sizes[index], RELAYED[index]
        others = [(j, 0, size) for j in range(far)]
        if relayed < size:
            others.append((far, relayed, size - relayed))
        return [(far, 0, relayed)], others

    def half_the_way(piece):
        return passed_along(piece, "pair", -(back - back // 2))

    def sent(pieces):
        moved = [passed_along(piece, "pair", offsets[min(j, far)]) for j, piece in enumerate(pieces)]
        return moved[:far], moved[far:]

    def rest_of_the_way(half_way):
        return passed_along(half_way, "pair", -(back // 2))

    outgoing = outgoing_parts(counts, documents)
    slab_0 = exchanged(outgoing[0])
    slab_1 = exchanged(outgoing[1])
    long_way, others = pieces_of(0)
    long_way, *others = cut(neighbours, slab_0, long_way + others, sizes[0], [])
    half_way = half_the_way(long_way)
    near_0, direct_0 = sent(others)
    far_0 = [rest_of_the_way(half_way)] + direct_0
    arrived = sum(block[:16, :128] for block in [half_way] + near_0)
    long_way, others = pieces_of(1)
    long_way, *others = cut(neighbours, slab_1, long_way + others, sizes[1], [arrived])
    near_1, direct_1 = sent(others)
    long_way, far_0[0] = lax.optimization_barrier((long_way, far_0[0]))
    half_way = half_the_way(long_way)
    slab_parts = [slab_0, slab_1]
    slab_best, blocks_0, row_bias = fold_blocks(slab_parts, near_0 + far_0, (), "early_scores")
    *near_1, _ = lax.optimization_barrier((*near_1, half_way))
    half_way, blocks_0 = lax.optimization_barrier((half_way, blocks_0))
    far_1 = [rest_of_the_way(half_way)] + direct_1
    slab_best, blocks_1 = fold_blocks(slab_parts, near_1, (row_bias, slab_best), "near_scores")
    slab_best, far_best = fold_blocks(slab_parts, far_1, (row_bias, slab_best), "last_scores")
    blocks_1, far_best = lax.optimization_barrier((blocks_1, far_best))
    blocks_1 = [blocks_1[:, j * sizes[1] : (j + 1) * sizes[1]] for j in range(far)] + [far_best]
    returned = [
        passed_along(
            jnp.concatenate([blocks_0[:, j * sizes[0] : (j + 1) * sizes[0]], blocks_1[j]], axis=1),
            "pair",
            -offsets[j],
        )
        for j in range(NEIGHBOURS)
    ]

    block_number = jnp.arange(lanes, dtype=jnp.int32)[:, None]
    pieces = []
    slot = 0
    for width, size in zip(WIDTHS, sizes):
        best = slab_best[0, slot * lanes : (slot + size) * lanes].reshape(lanes, size)
        for j in range(NEIGHBOURS):
            here = returned[j][:, slot : slot + size]
            listed = block_number == neighbours[:, j : j + 1]
            best = jnp.maximum(best, jnp.where(listed, here, FLOOR * 1024.0))
        pieces.append(best.reshape(dp_count, width))
        slot += size
    best = jnp.concatenate(pieces, axis=1)
    answers = lax.all_to_all(best, "dp", split_axis=0, concat_axis=0, tiled=True)
    found = pl.pallas_call(
        answer_kernel,
        out_shape=jax.ShapeDtypeStruct((1, row_count), jnp.float32),
        compiler_params=pltpu.CompilerParams(vmem_limit_bytes=24 * MEBIBYTE),
        name="answer",
    )(counts, answers)
    return found.reshape(row_count)


def solution(mesh):
    return jax.shard_map(
        body,
        mesh=mesh,
        in_specs=(P(("dp", "pair"), None), P(("dp", "pair"), None), P(("dp", "pair"), None)),
        out_specs=P(("dp", "pair")),
        check_vma=False,
    )
```

```python
import functools

import jax
import jax.numpy as jnp
from jax import lax
from jax.experimental import pallas as pl
from jax.experimental.pallas import tpu as pltpu
from jax.sharding import PartitionSpec as P

BLOCK = 512
NEIGHBOURS = 3
SLAB = 2048
WIDTHS = (16, 16)
RELAYED = (256, 160)
PARTS = len(WIDTHS)
CHUNK = 256
FLOOR = -2.0
DEAD = -1e9
MARK = 64.0
MEBIBYTE = 1024 * 1024
MOST_VMEM = 60 * MEBIBYTE

NT = (((1,), (1,)), ((), ()))


def column_starts(counts_row, owner_column):
    owners = lax.broadcasted_iota(jnp.int32, (owner_column.shape[0], counts_row.shape[1]), 1)
    before = jnp.sum(jnp.where(owners < owner_column, counts_row, 0.0), axis=1, keepdims=True)
    own = jnp.sum(jnp.where(owners == owner_column, counts_row, 0.0), axis=1, keepdims=True)
    return before, own


def picked_rows(counts_row, unit_ref, start, tile, first, width):
    slot = lax.broadcasted_iota(jnp.int32, (tile, 1), 0) + start
    owner = lax.shift_right_logical(slot, width.bit_length() - 1)
    rank = (lax.bitwise_and(slot, width - 1) + first).astype(jnp.float32)
    before, own = column_starts(counts_row, owner)
    live = rank < own
    wanted = jnp.where(live, before + rank, -1.0).astype(jnp.int32)
    lane = lax.broadcasted_iota(jnp.int32, (tile, unit_ref.shape[0]), 1)
    choice = jnp.where(lane == wanted, 1.0, 0.0).astype(jnp.bfloat16)
    picked = jnp.dot(choice, unit_ref[...], preferred_element_type=jnp.float32)
    place = lax.broadcasted_iota(jnp.int32, (tile, picked.shape[1]), 1)
    return jnp.where((place == 0) & (wanted < 0), MARK, picked).astype(jnp.bfloat16)


def first_kernel(counts_ref, documents_ref, unit_out, part_out, raw, unit, part, in_sem, unit_sem, part_sem, *, width):
    tile = 128
    steps = raw.shape[0] // tile
    loads = []
    for step in range(steps):
        here = pl.ds(step * tile, tile)
        loads.append(pltpu.make_async_copy(documents_ref.at[here], raw.at[here], in_sem.at[step]))
        loads[-1].start()
    for step in range(steps):
        here = pl.ds(step * tile, tile)
        loads[step].wait()
        values = raw[here, :].astype(jnp.float32)
        mean = jnp.mean(values * values, axis=-1, keepdims=True)
        unit[here, :] = (values * lax.rsqrt(mean + 1e-06)).astype(jnp.bfloat16)
    stores = [pltpu.make_async_copy(unit, unit_out, unit_sem)]
    stores[-1].start()
    counts_row = counts_ref[...].astype(jnp.float32)
    tile = 256
    for step in range(part.shape[0] // tile):
        here = pl.ds(step * tile, tile)
        part[here, :] = picked_rows(counts_row, unit, step * tile, tile, 0, width)
        stores.append(pltpu.make_async_copy(part.at[here], part_out.at[here], part_sem.at[step]))
        stores[-1].start()
    for store in stores:
        store.wait()


def later_kernel(counts_ref, unit_ref, out_ref, *, first, width):
    counts_row = counts_ref[...].astype(jnp.float32)
    tile = 256

    @pl.loop(0, out_ref.shape[0] // tile)
    def _(step):
        here = pl.ds(pl.multiple_of(step * tile, tile), tile)
        out_ref[here, :] = picked_rows(counts_row, unit_ref, step * tile, tile, first, width)


def outgoing_parts(counts, documents):
    owners = counts.shape[1]
    rows, feats = documents.shape
    width = WIDTHS[0]
    size = owners * width
    shape = lambda n: jax.ShapeDtypeStruct((n, feats), jnp.bfloat16)
    cost = lambda n: pl.CostEstimate(
        flops=2 * n * rows * feats, bytes_accessed=2 * (n + rows) * feats, transcendentals=0
    )
    whole = pl.BlockSpec(memory_space=pltpu.VMEM)
    anywhere = pl.BlockSpec(memory_space=pltpu.HBM)
    unit, part = pl.pallas_call(
        functools.partial(first_kernel, width=width),
        out_shape=(shape(rows), shape(size)),
        in_specs=[whole, anywhere],
        out_specs=(anywhere, anywhere),
        scratch_shapes=[
            pltpu.VMEM((rows, feats), jnp.bfloat16),
            pltpu.VMEM((rows, feats), jnp.bfloat16),
            pltpu.VMEM((size, feats), jnp.bfloat16),
            pltpu.SemaphoreType.DMA((rows // 128,)),
            pltpu.SemaphoreType.DMA,
            pltpu.SemaphoreType.DMA((size // 256,)),
        ],
        compiler_params=pltpu.CompilerParams(vmem_limit_bytes=MOST_VMEM),
        cost_estimate=cost(size),
        name="unit_and_pick",
    )(counts, documents)
    parts = [part]
    first = width
    for width in WIDTHS[1:]:
        parts.append(
            pl.pallas_call(
                functools.partial(later_kernel, first=first, width=width),
                out_shape=shape(owners * width),
                in_specs=[whole, whole],
                out_specs=whole,
                compiler_params=pltpu.CompilerParams(vmem_limit_bytes=24 * MEBIBYTE),
                cost_estimate=cost(owners * width),
                name="pick",
            )(counts, unit)
        )
        first += width
    return parts


def score_tile(scores, row_bias, column_bias, best_ref, rows):
    live = scores + row_bias
    part = best_ref[rows, :]
    for lane in range(0, scores.shape[1], 128):
        part = jnp.maximum(part, live[:, lane : lane + 128])
    best_ref[rows, :] = part
    return jnp.max(scores + column_bias, axis=0, keepdims=True)


def block_bias(block):
    return jnp.where(block[:, 0:1].astype(jnp.float32) > 0.75 * MARK, DEAD, 0.0)


def best_row(best_ref, rows):
    turned = best_ref[rows, :].T
    return jnp.max(turned, axis=0, keepdims=True)


def row_offsets(refs):
    offsets = [0]
    for ref in refs:
        offsets.append(offsets[-1] + ref.shape[0])
    return offsets


def loads_of(refs, target, sems):
    offsets = row_offsets(refs)
    return [
        pltpu.make_async_copy(ref, target.at[pl.ds(offset, ref.shape[0])], sems.at[i])
        for i, (ref, offset) in enumerate(zip(refs, offsets))
    ]


TILE = 256


def tile_load(slab_ref, offset, step, slab, sems):
    rows = pl.ds(pl.multiple_of(step * TILE, TILE), TILE)
    there = pl.ds(pl.multiple_of(offset + step * TILE, TILE), TILE)
    return pltpu.make_async_copy(slab_ref.at[rows], slab.at[there], sems.at[offset // TILE + step])


def fold_scores(slab_refs, slab, slab_sem, blocks, best, row_bias_of, slab_best_of, slab_best_ref):
    for slab_ref, offset in zip(slab_refs, row_offsets(slab_refs)):

        @pl.loop(0, slab_ref.shape[0] // TILE)
        def _(step, slab_ref=slab_ref, offset=offset):
            tile_load(slab_ref, offset, step, slab, slab_sem).wait()
            there = pl.ds(pl.multiple_of(offset + step * TILE, TILE), TILE)
            here = slab[there, :]
            row_bias = row_bias_of(there, here)
            slab_best = slab_best_of(there)
            for begin in range(0, blocks.shape[0], CHUNK):
                rows = pl.ds(begin, CHUNK)
                block = blocks[rows, :]
                scores = lax.dot_general(block, here, NT, preferred_element_type=jnp.float32)
                slab_best = jnp.maximum(
                    slab_best, score_tile(scores, row_bias, block_bias(block), best, rows)
                )
            slab_best_ref[:, there] = slab_best

    return jnp.concatenate(
        [best_row(best, pl.ds(begin, CHUNK)) for begin in range(0, blocks.shape[0], CHUNK)], axis=1
    )


def score_kernel(*refs, count, first):
    slab_refs, block_refs = refs[:PARTS], refs[PARTS : PARTS + count]
    refs = refs[PARTS + count :]
    if first:
        slab_best_ref, block_best_ref, row_bias_ref, slab, blocks, best, slab_sem, block_sem = refs
    else:
        row_bias_ref, before_ref, slab_best_ref, block_best_ref, slab, blocks, best, slab_sem, block_sem = refs
    block_loads = loads_of(block_refs, blocks, block_sem)
    for load in block_loads:
        load.start()
    for slab_ref, offset in zip(slab_refs, row_offsets(slab_refs)):
        for step in range(slab_ref.shape[0] // TILE):
            tile_load(slab_ref, offset, step, slab, slab_sem).start()
    best[...] = jnp.full(best.shape, 4 * DEAD, jnp.float32)
    for load in block_loads:
        load.wait()

    def row_bias_of(there, here):
        if not first:
            return row_bias_ref[:, there]
        marks = here[:, 0:128].astype(jnp.float32).T[0:1, :]
        row_bias = jnp.where(marks > 0.75 * MARK, DEAD, 0.0)
        row_bias_ref[:, there] = row_bias
        return row_bias

    def slab_best_of(there):
        if not first:
            return before_ref[:, there]
        return jnp.full((1, there.size), FLOOR * 1024.0, jnp.float32)

    block_best_ref[...] = fold_scores(
        slab_refs, slab, slab_sem, blocks, best, row_bias_of, slab_best_of, slab_best_ref
    )


def fold_blocks(slab_parts, blocks, before, name):
    feats = slab_parts[0].shape[1]
    whole = pl.BlockSpec(memory_space=pltpu.VMEM)
    anywhere = pl.BlockSpec(memory_space=pl.ANY)
    total = sum(block.shape[0] for block in blocks)
    row = lambda n: jax.ShapeDtypeStruct((1, n), jnp.float32)
    shapes = (row(SLAB), row(total)) if before else (row(SLAB), row(total), row(SLAB))
    return pl.pallas_call(
        functools.partial(score_kernel, count=len(blocks), first=not before),
        out_shape=shapes,
        in_specs=[anywhere] * (PARTS + len(blocks)) + [whole] * len(before),
        out_specs=(whole,) * len(shapes),
        scratch_shapes=[
            pltpu.VMEM((SLAB, feats), jnp.bfloat16),
            pltpu.VMEM((total, feats), jnp.bfloat16),
            pltpu.VMEM((total, 128), jnp.float32),
            pltpu.SemaphoreType.DMA((SLAB // TILE,)),
            pltpu.SemaphoreType.DMA((len(blocks),)),
        ],
        compiler_params=pltpu.CompilerParams(vmem_limit_bytes=24 * MEBIBYTE),
        cost_estimate=pl.CostEstimate(
            flops=2 * SLAB * total * feats, bytes_accessed=2 * (SLAB + total) * feats, transcendentals=0
        ),
        name=name,
    )(*slab_parts, *blocks, *before)


def cut_kernel(chosen_ref, slab_ref, *refs, pieces, size):
    outs = refs[-3 - len(pieces) : -3]
    staged, load_sem, store_sem = refs[-3:]
    loads, stores = [], []
    offset = 0
    for index, (j, begin, rows) in enumerate(pieces):
        start = pl.multiple_of(chosen_ref[0, j] * size + begin, 16)
        stage = staged.at[pl.ds(offset, rows)]
        loads.append(pltpu.make_async_copy(slab_ref.at[pl.ds(start, rows)], stage, load_sem.at[index]))
        stores.append(pltpu.make_async_copy(stage, outs[index], store_sem.at[index]))
        loads[-1].start()
        offset += rows
    for load, store in zip(loads, stores):
        load.wait()
        store.start()
    for store in stores:
        store.wait()


def cut(neighbours, slab_part, pieces, size, after):
    feats = slab_part.shape[1]
    anywhere = pl.BlockSpec(memory_space=pl.ANY)
    return pl.pallas_call(
        functools.partial(cut_kernel, pieces=pieces, size=size),
        out_shape=tuple(jax.ShapeDtypeStruct((rows, feats), slab_part.dtype) for _, _, rows in pieces),
        in_specs=[pl.BlockSpec(memory_space=pltpu.SMEM)] + [anywhere] * (1 + len(after)),
        out_specs=(anywhere,) * len(pieces),
        scratch_shapes=[
            pltpu.VMEM((sum(rows for _, _, rows in pieces), feats), slab_part.dtype),
            pltpu.SemaphoreType.DMA((len(pieces),)),
            pltpu.SemaphoreType.DMA((len(pieces),)),
        ],
        compiler_params=pltpu.CompilerParams(vmem_limit_bytes=MOST_VMEM if after else 4 * MEBIBYTE),
        cost_estimate=pl.CostEstimate(flops=0, bytes_accessed=8 * size * feats, transcendentals=0),
        name="cut",
    )(neighbours, slab_part, *after)


def answer_kernel(counts_ref, answers_ref, out_ref):
    counts_row = counts_ref[...].astype(jnp.float32)
    owners, capacity = answers_ref.shape
    docs = out_ref.shape[1]
    owner = lax.broadcasted_iota(jnp.int32, (owners, 1), 0)
    before, own = column_starts(counts_row, owner)
    position = lax.broadcasted_iota(jnp.int32, (owners, docs), 1).astype(jnp.float32)
    mine = (position >= before) & (position < before + own)
    start = jnp.sum(jnp.where(mine, before, 0.0), axis=0, keepdims=True)
    rank = (position[:1] - start).astype(jnp.int32)
    spread = lax.dot_general(
        answers_ref[...],
        jnp.where(mine, 1.0, 0.0),
        (((0,), (0,)), ((), ())),
        precision=lax.Precision.HIGHEST,
        preferred_element_type=jnp.float32,
    )
    ranks = lax.broadcasted_iota(jnp.int32, (capacity, docs), 0)
    found = jnp.sum(jnp.where(ranks == rank, spread, 0.0), axis=0, keepdims=True)
    out_ref[...] = found * (1.0 / 1024.0)


def passed_along(x, axis, by):
    length = lax.axis_size(axis)
    return lax.ppermute(x, axis, [(i, (i + by) % length) for i in range(length)])


def body(documents, counts, neighbours):
    dp_count = lax.axis_size("dp")
    pair_count = lax.axis_size("pair")
    row_count, feats = documents.shape
    capacity = SLAB // dp_count
    lanes = SLAB // BLOCK
    sources = dp_count // lanes
    offsets = [1 + j % (pair_count - 1) for j in range(NEIGHBOURS)]

    sizes = [sources * width for width in WIDTHS]
    far = NEIGHBOURS - 1
    back = pair_count - offsets[far]

    def exchanged(part):
        return lax.all_to_all(part, "dp", split_axis=0, concat_axis=0, tiled=True)

    def pieces_of(index):
        size, relayed = sizes[index], RELAYED[index]
        others = [(j, 0, size) for j in range(far)]
        if relayed < size:
            others.append((far, relayed, size - relayed))
        return [(far, 0, relayed)], others

    def half_the_way(piece):
        return passed_along(piece, "pair", -(back - back // 2))

    def sent(pieces):
        moved = [passed_along(piece, "pair", offsets[min(j, far)]) for j, piece in enumerate(pieces)]
        return moved[:far], moved[far:]

    def rest_of_the_way(half_way):
        return passed_along(half_way, "pair", -(back // 2))

    outgoing = outgoing_parts(counts, documents)
    slab_0 = exchanged(outgoing[0])
    slab_1 = exchanged(outgoing[1])
    long_way, others = pieces_of(0)
    long_way, *others = cut(neighbours, slab_0, long_way + others, sizes[0], [])
    half_way = half_the_way(long_way)
    near_0, direct_0 = sent(others)
    far_0 = [rest_of_the_way(half_way)] + direct_0
    arrived = sum(block[:16, :128] for block in [half_way] + near_0)
    long_way, others = pieces_of(1)
    long_way, *others = cut(neighbours, slab_1, long_way + others, sizes[1], [arrived])
    near_1, direct_1 = sent(others)
    long_way, far_0[0] = lax.optimization_barrier((long_way, far_0[0]))
    half_way = half_the_way(long_way)
    slab_parts = [slab_0, slab_1]
    slab_best, blocks_0, row_bias = fold_blocks(slab_parts, near_0 + far_0, (), "early_scores")
    *near_1, _ = lax.optimization_barrier((*near_1, half_way))
    half_way, blocks_0 = lax.optimization_barrier((half_way, blocks_0))
    far_1 = [rest_of_the_way(half_way)] + direct_1
    slab_best, blocks_1 = fold_blocks(slab_parts, near_1, (row_bias, slab_best), "near_scores")
    slab_best, far_best = fold_blocks(slab_parts, far_1, (row_bias, slab_best), "last_scores")
    blocks_1 = [blocks_1[:, j * sizes[1] : (j + 1) * sizes[1]] for j in range(far)] + [far_best]
    returned = [
        passed_along(
            jnp.concatenate([blocks_0[:, j * sizes[0] : (j + 1) * sizes[0]], blocks_1[j]], axis=1),
            "pair",
            -offsets[j],
        )
        for j in range(NEIGHBOURS)
    ]

    block_number = jnp.arange(lanes, dtype=jnp.int32)[:, None]
    pieces = []
    slot = 0
    for width, size in zip(WIDTHS, sizes):
        best = slab_best[0, slot * lanes : (slot + size) * lanes].reshape(lanes, size)
        for j in range(NEIGHBOURS):
            here = returned[j][:, slot : slot + size]
            listed = block_number == neighbours[:, j : j + 1]
            best = jnp.maximum(best, jnp.where(listed, here, FLOOR * 1024.0))
        pieces.append(best.reshape(dp_count, width))
        slot += size
    best = jnp.concatenate(pieces, axis=1)
    answers = lax.all_to_all(best, "dp", split_axis=0, concat_axis=0, tiled=True)
    found = pl.pallas_call(
        answer_kernel,
        out_shape=jax.ShapeDtypeStruct((1, row_count), jnp.float32),
        compiler_params=pltpu.CompilerParams(vmem_limit_bytes=24 * MEBIBYTE),
        name="answer",
    )(counts, answers)
    return found.reshape(row_count)


def solution(mesh):
    return jax.shard_map(
        body,
        mesh=mesh,
        in_specs=(P(("dp", "pair"), None), P(("dp", "pair"), None), P(("dp", "pair"), None)),
        out_specs=P(("dp", "pair")),
        check_vma=False,
    )
```
